256 devices in a mesh: streams: 64 (over z, y, core), mp: 4 (over x).
Axes of the slice: x: 4, y: 4, z: 8, core: 2. Of those that a mesh axis runs over, the one named last changes fastest.
Arguments:
- features: float32 [1024, 1280], P('streams'), may hold values from -6 to 6
- block_valid_frames: int32 [1024], P('streams'), may hold values from 1 to 16
- feature_running_mean: float32 [1024, 80], P('streams'), may hold values from -4 to 4
- feature_running_variance: float32 [1024, 80], P('streams'), may hold values from 0.3 to 3
- frames_counted: float32 [1024], P('streams'), may hold values from 4 to 128
- slot_relocation: int32 [1024], replicated, may hold values from 0 to 1023, as said below
- speaker: int32 [1024], replicated, may hold values from 0 to 255, as said below
- speaker_adapter_row: int32 [256], replicated, may hold values from 0 to 255, as said below
- adapter_down_panels: bfloat16 [256, 32, 80], P('streams'), may hold values from -0.625 to 0.625
- adapter_up_panels: bfloat16 [256, 32, 768], P('streams', None, 'mp'), may hold values from -1 to 1
- input_weight: bfloat16 [80, 768], P(None, 'mp'), may hold values from -0.625 to 0.625
- attention_norm_gain: float32 [2, 768], P(None, 'mp'), may hold values from 0.25 to 1.75
- query_key_value_weight: bfloat16 [2, 768, 3, 768], P(None, None, None, 'mp'), may hold values from -0.21875 to 0.21875
- attention_output_weight: bfloat16 [2, 768, 768], P(None, 'mp'), may hold values from -0.21875 to 0.21875
- convolution_norm_gain: float32 [2, 768], P(None, 'mp'), may hold values from 0.25 to 1.75
- depthwise_taps: float32 [2, 31, 768], P(None, None, 'mp'), may hold values from -1 to 1
- feedforward_norm_gain: float32 [2, 768], P(None, 'mp'), may hold values from 0.25 to 1.75
- up_weight: bfloat16 [2, 768, 1536], P(None, None, 'mp'), may hold values from -0.21875 to 0.21875
- down_weight: bfloat16 [2, 1536, 768], P(None, 'mp'), may hold values from -0.15625 to 0.15625
- key_value_cache: bfloat16 [1024, 2, 64, 12, 128], P('streams', None, None, 'mp'), may hold values from -140 to 140
- convolution_cache: bfloat16 [1024, 2, 30, 768], P('streams', None, None, 'mp'), may hold values from -6 to 6
Outputs:
- enc_out: bfloat16 [768, 16384], P('mp', 'streams')
- new_kv: bfloat16 [1024, 2, 64, 12, 128], P('streams', None, None, 'mp')
- new_conv: bfloat16 [1024, 2, 30, 768], P('streams', None, None, 'mp')
- new_mean: float32 [1024, 80], P('streams')
- new_var: float32 [1024, 80], P('streams')
The draws below stay inside these ranges and needn't reach their ends.
Inputs may be any that keep to these rules, and one draw needn't show every extreme that they name: A permutation of the 1024 slots: old slot i is held by device i // 16 of streams and its stream moves to new slot slot_relocation[i], held by device slot_relocation[i] // 16. Of one device's 16 old slots at most 1 go to any one device, and exactly 1 go to some device. A permutation: speaker s has its panels in row speaker_adapter_row[s] of adapter_down_panels and adapter_up_panels, held by device speaker_adapter_row[s] // 4 of streams. `speaker`: among the 16 new slots of one device, at most 1 have their panel row held by any one device of streams, and exactly 1 by some device.
All inputs are finite; a program needn't handle non-finite values.
Results may differ from the reference program's by a relative error of at most 0.019.
Values may be sent and summed in bfloat16 or wider, within the bound.
No kernel may reach another device: no remote copies, remote signals or barrier semaphores. Data moves between devices by JAX's collectives and lax.ppermute only.
A program may use at most 128 MiB of HBM per device.

```python
import math
import jax
import jax.numpy as jnp
from jax import lax

MODEL_WIDTH = 768
HEADS = 12
HEAD_DIM = 64
FF = 1536
FILTER_CHANNELS = 80
ADAPTER_RANK = 32
FR = 64
KT = 31
CH = 16
LAYERS = 2
S_DEV = 16
SPK_DEV = 4
SLOT_CAP = 1
STREAMS = 1024
SPEAKER_COUNT = 256
ROWS = 16384
N_STREAMS = 64


def spread_targets(key):
    key_labels, key_tickets = jax.random.split(key)
    labels = jax.random.permutation(key_labels, N_STREAMS)
    places = jnp.argsort(labels)
    tickets = jax.random.permutation(key_tickets, N_STREAMS * SLOT_CAP)[:S_DEV]
    offsets = tickets // SLOT_CAP
    return labels[(places[:, None] + offsets[None, :]) % N_STREAMS]


def row_orders(key):
    return jax.vmap(lambda single: jax.random.permutation(single, S_DEV))(jax.random.split(key, N_STREAMS))


def panel_table(key):
    return jax.random.permutation(jax.random.fold_in(key, 101), SPEAKER_COUNT).astype(jnp.int32)


def draw_slot_relocation(key, part):
    key = jax.random.fold_in(key, 3)
    key_spread, key_old, key_new = jax.random.split(key, 3)
    targets = spread_targets(key_spread)
    old_local = row_orders(key_old)
    new_local = row_orders(key_new)
    arrival = new_local[targets, jnp.arange(S_DEV)[None, :]]
    sources = (jnp.arange(N_STREAMS)[:, None] * S_DEV + old_local).reshape(-1)
    settled = (targets * S_DEV + arrival).reshape(-1).astype(jnp.int32)
    return jnp.zeros((STREAMS,), jnp.int32).at[sources].set(settled)


def draw_speaker_adapter_row(key, part):
    return panel_table(key)


def draw_speaker(key, part):
    table = panel_table(key)
    key = jax.random.fold_in(key, 5)
    key_spread, key_local = jax.random.split(key)
    owners = spread_targets(key_spread)
    local_rows = jax.random.randint(key_local, (N_STREAMS, S_DEV), 0, SPK_DEV)
    rows_all = (owners * SPK_DEV + local_rows).reshape(-1)
    return jnp.argsort(table)[rows_all].astype(jnp.int32)


def draw_key_value_cache(key, part):
    key = jax.random.fold_in(key, 7)
    key_base = jax.random.fold_in(key, 0)
    shape = (STREAMS, LAYERS, FR, HEADS, 2 * HEAD_DIM)
    values = jnp.clip(jax.random.normal(key_base, shape, jnp.float32), -6.0, 6.0)
    return values.astype(jnp.bfloat16)


def touch_ends(values, key, least, top_value):
    longest = values.shape.index(max(values.shape))
    spots = []
    for shift in (0, 1):
        where = [jax.random.randint(jax.random.fold_in(key, axis), (), 0, length) for axis, length in enumerate(values.shape)]
        where[longest] = (where[longest] + shift) % values.shape[longest]
        spots.append(tuple(where))
    return values.at[spots[0]].set(least).at[spots[1]].set(top_value)


def block_levels(key, extent, cuts, smallest, top_value):
    level = 1.0
    for position, shards_of in cuts:
        heights = jax.random.uniform(jax.random.fold_in(jax.random.fold_in(key, 6), position), (shards_of,), jnp.float32, smallest / len(cuts), top_value / len(cuts))
        level = level * jnp.repeat(jnp.exp(heights), extent[position] // shards_of).reshape((-1,) + (1,) * (len(extent) - 1 - position))
    return level


def normal_values(own_key, dims, deviation, limit, cuts=(), held_as=jnp.bfloat16):
    result = jax.random.normal(own_key, dims, jnp.float32) * deviation
    if len(cuts) > 0:
        result = block_levels(own_key, dims, cuts, -0.22, 0.18) * result
    return jnp.clip(result, min=-limit, max=limit).astype(held_as)


def setup_inputs(seed: int = 0) -> dict:
    streams_of = jax.random.split(jax.random.key(seed), 22)
    return {
        "features": normal_values(streams_of[0], (STREAMS, CH * FILTER_CHANNELS), 1.0, 6.0, ((0, 64),), jnp.float32),
        "block_valid_frames": touch_ends(jax.random.randint(streams_of[1], (STREAMS,), 1, CH + 1), jax.random.fold_in(streams_of[1], 1), 1, CH).astype(jnp.int32),
        "feature_running_mean": normal_values(streams_of[2], (STREAMS, FILTER_CHANNELS), 0.7, 4.0, ((0, 64),), jnp.float32),
        "feature_running_variance": jnp.clip(jnp.exp(math.log(3.0) - 2.3025851 * jax.random.uniform(streams_of[3], (STREAMS, FILTER_CHANNELS), jnp.float32) ** block_levels(streams_of[3], (STREAMS, FILTER_CHANNELS), ((0, 64),), -0.2, 0.2)), 0.3, 3.0),
        "frames_counted": jnp.clip(jnp.exp(math.log(128.0) - 3.465736 * jax.random.uniform(streams_of[4], (STREAMS,), jnp.float32) ** block_levels(streams_of[4], (STREAMS,), ((0, 64),), -0.2, 0.2)), 4.0, 128.0),
        "slot_relocation": draw_slot_relocation(jax.random.fold_in(streams_of[21], 71), 0),
        "speaker": draw_speaker(jax.random.fold_in(streams_of[21], 71), 0),
        "speaker_adapter_row": draw_speaker_adapter_row(jax.random.fold_in(streams_of[21], 71), 0),
        "adapter_down_panels": normal_values(streams_of[8], (SPEAKER_COUNT, ADAPTER_RANK, FILTER_CHANNELS), FILTER_CHANNELS ** -0.5, 0.625, ((0, 64),)),
        "adapter_up_panels": normal_values(streams_of[9], (SPEAKER_COUNT, ADAPTER_RANK, MODEL_WIDTH), ADAPTER_RANK ** -0.5, 1.0, ((0, 64), (2, 4))),
        "input_weight": normal_values(streams_of[10], (FILTER_CHANNELS, MODEL_WIDTH), FILTER_CHANNELS ** -0.5, 0.625, ((1, 4),)),
        "attention_norm_gain": jnp.clip(1.0 + 0.15 * jax.random.normal(streams_of[11], (LAYERS, MODEL_WIDTH), jnp.float32), 0.25, 1.75),
        "query_key_value_weight": normal_values(streams_of[12], (LAYERS, MODEL_WIDTH, 3, MODEL_WIDTH), MODEL_WIDTH ** -0.5, 0.21875, ((3, 4),)),
        "attention_output_weight": normal_values(streams_of[13], (LAYERS, MODEL_WIDTH, MODEL_WIDTH), MODEL_WIDTH ** -0.5, 0.21875, ((1, 4),)),
        "convolution_norm_gain": jnp.clip(1.0 + 0.15 * jax.random.normal(streams_of[14], (LAYERS, MODEL_WIDTH), jnp.float32), 0.25, 1.75),
        "depthwise_taps": normal_values(streams_of[15], (LAYERS, KT, MODEL_WIDTH), KT ** -0.5, 1.0, ((2, 4),), jnp.float32),
        "feedforward_norm_gain": jnp.clip(1.0 + 0.15 * jax.random.normal(streams_of[16], (LAYERS, MODEL_WIDTH), jnp.float32), 0.25, 1.75),
        "up_weight": normal_values(streams_of[17], (LAYERS, MODEL_WIDTH, FF), MODEL_WIDTH ** -0.5, 0.21875, ((2, 4),)),
        "down_weight": normal_values(streams_of[18], (LAYERS, FF, MODEL_WIDTH), FF ** -0.5, 0.15625, ((1, 4),)),
        "key_value_cache": draw_key_value_cache(jax.random.fold_in(streams_of[21], 71), 0),
        "convolution_cache": normal_values(streams_of[20], (STREAMS, LAYERS, KT - 1, MODEL_WIDTH), 1.0, 6.0, ((0, 64), (3, 4))),
    }


NORM_EPS = 1e-06
CMVN_EPS = 1e-05

def scaled_rows(values, gain):
    spread = jnp.sqrt(lax.optimization_barrier(jnp.mean(values * values, axis=-1, keepdims=True)) + NORM_EPS)
    return (values / spread * gain).astype(jnp.bfloat16)

def window(frames, block_valid_frames, length):
    picks = block_valid_frames[:, None] + jnp.arange(length, dtype=jnp.int32)[None, :]
    picks = picks.reshape(picks.shape + (1,) * (frames.ndim - 2))
    return jnp.take_along_axis(frames, picks, axis=1)

def encoder_stream_step(feature_block, block_valid_frames, feature_running_mean, feature_running_variance, frames_counted, panel_down, panel_up, kv_old, conv_old, input_weight, attention_norm_gain, query_key_value_weight, attention_output_weight, convolution_norm_gain, depthwise_taps, feedforward_norm_gain, up_weight, down_weight):
    streams_here = feature_block.shape[0]
    frames = feature_block.reshape(streams_here, CH, FILTER_CHANNELS)
    positions = jnp.arange(CH, dtype=jnp.int32)
    live = (positions[None, :] < block_valid_frames[:, None]).astype(jnp.float32)[:, :, None]
    seen_here = frames_counted[:, None]
    counted = seen_here + block_valid_frames.astype(jnp.float32)[:, None]
    new_mean = (seen_here * feature_running_mean + lax.optimization_barrier(jnp.sum(live * frames, axis=1))) / counted
    centred = frames - new_mean[:, None, :]
    shifted = feature_running_mean - new_mean
    new_var = (seen_here * (feature_running_variance + shifted * shifted) + lax.optimization_barrier(jnp.sum(live * centred * centred, axis=1))) / counted
    normed = (centred / jnp.sqrt(new_var + CMVN_EPS)[:, None, :]).astype(jnp.bfloat16)
    state = jnp.dot(normed.reshape(streams_here * CH, FILTER_CHANNELS), input_weight, preferred_element_type=jnp.float32).reshape(streams_here, CH, MODEL_WIDTH)
    low = jnp.einsum('btm,brm->btr', normed.astype(jnp.float32), panel_down.astype(jnp.float32)).astype(jnp.bfloat16)
    state = state + jnp.einsum('btr,brd->btd', low.astype(jnp.float32), panel_up.astype(jnp.float32))
    columns = jnp.arange(FR + CH, dtype=jnp.int32)
    fresh = columns - FR
    allowed = (columns[None, None, :] < FR) | (fresh[None, None, :] <= positions[None, :, None]) & (fresh[None, None, :] < block_valid_frames[:, None, None])
    kv_layers = []
    conv_layers = []
    for layer_index in range(LAYERS):
        attn_in = scaled_rows(state, attention_norm_gain[layer_index])
        qkv = jnp.dot(attn_in.reshape(streams_here * CH, MODEL_WIDTH), query_key_value_weight[layer_index].reshape(MODEL_WIDTH, 3 * MODEL_WIDTH), preferred_element_type=jnp.float32)
        qkv = qkv.astype(jnp.bfloat16).reshape(streams_here, CH, 3, HEADS, HEAD_DIM)
        cached = kv_old[:, layer_index]
        keys = jnp.concatenate([cached[..., :HEAD_DIM], qkv[:, :, 1]], axis=1)
        vals = jnp.concatenate([cached[..., HEAD_DIM:], qkv[:, :, 2]], axis=1)
        scores = jnp.einsum('bthe,bshe->bhts', qkv[:, :, 0].astype(jnp.float32), keys.astype(jnp.float32)) * HEAD_DIM ** (-0.5)
        scores = jnp.where(allowed[:, None], scores, -1e+30)
        peak = lax.optimization_barrier(jnp.max(scores, axis=-1, keepdims=True))
        weights = jnp.exp(scores - peak)
        probs = (weights / lax.optimization_barrier(jnp.sum(weights, axis=-1, keepdims=True))).astype(jnp.bfloat16)
        heads_out = jnp.einsum('bhts,bshe->bthe', probs.astype(jnp.float32), vals.astype(jnp.float32)).astype(jnp.bfloat16)
        state = state + jnp.dot(heads_out.reshape(streams_here * CH, MODEL_WIDTH), attention_output_weight[layer_index], preferred_element_type=jnp.float32).reshape(streams_here, CH, MODEL_WIDTH)
        kv_layers.append(window(jnp.concatenate([keys, vals], axis=-1), block_valid_frames, FR))
        conv_in = scaled_rows(state, convolution_norm_gain[layer_index])
        comb = jnp.concatenate([conv_old[:, layer_index], conv_in], axis=1)
        mixed = jnp.zeros((streams_here, CH, MODEL_WIDTH), jnp.float32)
        for tap in range(KT):
            mixed = mixed + depthwise_taps[layer_index, tap] * comb[:, tap:tap + CH].astype(jnp.float32)
        state = state + jax.nn.silu(mixed)
        conv_layers.append(window(comb, block_valid_frames, KT - 1))
        ffn_in = scaled_rows(state, feedforward_norm_gain[layer_index])
        hidden = jax.nn.silu(jnp.dot(ffn_in.reshape(streams_here * CH, MODEL_WIDTH), up_weight[layer_index], preferred_element_type=jnp.float32)).astype(jnp.bfloat16)
        state = state + jnp.dot(hidden, down_weight[layer_index], preferred_element_type=jnp.float32).reshape(streams_here, CH, MODEL_WIDTH)
    return (state.astype(jnp.bfloat16), jnp.stack(kv_layers, axis=1), jnp.stack(conv_layers, axis=1), new_mean, new_var)

def reference(features, block_valid_frames, feature_running_mean, feature_running_variance, frames_counted, slot_relocation, speaker, speaker_adapter_row, adapter_down_panels, adapter_up_panels, input_weight, attention_norm_gain, query_key_value_weight, attention_output_weight, convolution_norm_gain, depthwise_taps, feedforward_norm_gain, up_weight, down_weight, key_value_cache, convolution_cache):
    anchor = jnp.zeros((STREAMS,), jnp.int32).at[slot_relocation].set(jnp.arange(STREAMS, dtype=jnp.int32))
    panel_rows = speaker_adapter_row[speaker]

    def run_block(block_index):
        first = block_index * S_DEV

        def boundary_point(array):
            return lax.dynamic_slice_in_dim(array, first, S_DEV, 0)
        previous_slots = boundary_point(anchor)
        present_rows = boundary_point(panel_rows)
        return encoder_stream_step(boundary_point(features), boundary_point(block_valid_frames), boundary_point(feature_running_mean), boundary_point(feature_running_variance), boundary_point(frames_counted), adapter_down_panels[present_rows], adapter_up_panels[present_rows], key_value_cache[previous_slots], convolution_cache[previous_slots], input_weight, attention_norm_gain, query_key_value_weight, attention_output_weight, convolution_norm_gain, depthwise_taps, feedforward_norm_gain, up_weight, down_weight)
    results = lax.map(run_block, jnp.arange(N_STREAMS, dtype=jnp.int32))
    enc_out = jnp.transpose(results[0].reshape(ROWS, MODEL_WIDTH))
    new_kv = results[1].reshape((STREAMS,) + results[1].shape[2:])
    new_conv = results[2].reshape((STREAMS,) + results[2].shape[2:])
    new_mean = results[3].reshape(STREAMS, FILTER_CHANNELS)
    new_var = results[4].reshape(STREAMS, FILTER_CHANNELS)
    return (enc_out, new_kv, new_conv, new_mean, new_var)
```

```python
import jax
import jax.numpy as jnp
from jax import lax
from jax.sharding import PartitionSpec as P

MODEL_WIDTH = 768
HEAD_DIM = 64
FILTER_CHANNELS = 80
FR = 64
KT = 31
CH = 16
LAYERS = 2
MP = 4

NORM_EPS = 1e-06
CMVN_EPS = 1e-05


def from_peer(x, shift):
    return lax.ppermute(x, "mp", [((i + shift) % MP, i) for i in range(MP)])


def ring(x):
    return [x] + [from_peer(x, s) for s in range(1, MP)]


def norm(state, gain):
    total = jnp.sum(state * state, axis=-1, keepdims=True)
    spread = jnp.sqrt(total / MODEL_WIDTH + NORM_EPS)
    return (state / spread * gain).astype(jnp.bfloat16)


def dot(a, b):
    return lax.dot_general(a, b, (((1,), (0,)), ((), ())), preferred_element_type=jnp.float32)


def exchange(x):
    return lax.all_to_all(x, "streams", split_axis=0, concat_axis=0, tiled=True)


def window(frames, block_valid_frames, length):
    picks = block_valid_frames[:, None] + jnp.arange(length, dtype=jnp.int32)[None, :]
    picks = picks.reshape(picks.shape + (1,) * (frames.ndim - 2))
    return jnp.take_along_axis(frames, picks, axis=1)


def local(
    features,
    block_valid_frames,
    feature_running_mean,
    feature_running_variance,
    frames_counted,
    slot_relocation,
    speaker,
    speaker_adapter_row,
    adapter_down_panels,
    adapter_up_panels,
    input_weight,
    attention_norm_gain,
    query_key_value_weight,
    attention_output_weight,
    convolution_norm_gain,
    depthwise_taps,
    feedforward_norm_gain,
    up_weight,
    down_weight,
    key_value_cache,
    convolution_cache,
):
    slots = key_value_cache.shape[0]
    peers = lax.axis_size("streams")
    me = lax.axis_index("streams")
    mp = lax.axis_index("mp")
    first = me * slots
    total = slot_relocation.shape[0]
    held = adapter_down_panels.shape[0]
    width = input_weight.shape[1]
    heads = key_value_cache.shape[3]
    rows = slots * CH

    mine = jnp.arange(slots, dtype=jnp.int32)
    peer = jnp.arange(peers, dtype=jnp.int32)

    ids = jnp.arange(speaker_adapter_row.shape[0], dtype=jnp.int32)
    all_rows = jnp.sum(
        jnp.where(speaker[:, None] == ids[None, :], speaker_adapter_row[None, :], 0), axis=1
    )
    asked = all_rows.reshape(peers, slots)
    give = jnp.sum(jnp.where(asked // held == me, asked % held, 0), axis=1)
    my_rows = lax.dynamic_slice_in_dim(all_rows, first, slots, 0)
    got_down = exchange(jnp.take(adapter_down_panels, give, axis=0, mode="clip"))
    got_up = exchange(jnp.take(adapter_up_panels, give, axis=0, mode="clip"))
    panel_down = jnp.take(got_down, my_rows // held, axis=0, mode="clip")
    panel_up = jnp.take(got_up, my_rows // held, axis=0, mode="clip")

    targets = lax.dynamic_slice_in_dim(slot_relocation, first, slots, 0) // slots
    chosen = jnp.sum(jnp.where(peer[:, None] == targets[None, :], mine[None, :], 0), axis=1)
    anchor = jnp.sum(
        jnp.where(
            slot_relocation[None, :] == (first + mine)[:, None],
            jnp.arange(total, dtype=jnp.int32)[None, :],
            0,
        ),
        axis=1,
    )
    source = anchor // slots
    kv = jnp.transpose(key_value_cache, (1, 0, 3, 2, 4))
    kv_moved = []
    for layer in range(LAYERS):
        got = exchange(jnp.take(kv[layer], chosen, axis=0, mode="clip"))
        kv_moved.append(jnp.take(got, source, axis=0, mode="clip"))
    conv_got = exchange(jnp.take(convolution_cache, chosen, axis=0, mode="clip"))
    conv_own = jnp.take(conv_got, source, axis=0, mode="clip")
    conv_moved = lax.all_gather(conv_own, "mp", axis=3, tiled=True)

    small = jnp.concatenate(
        [
            attention_norm_gain,
            convolution_norm_gain,
            feedforward_norm_gain,
            depthwise_taps.reshape(LAYERS * KT, width),
        ],
        axis=0,
    )
    small = lax.all_gather(small, "mp", axis=1, tiled=True)
    attn_gain, conv_gain, ffn_gain = small[0:2], small[2:4], small[4:6]
    taps = small[6:].reshape(LAYERS, KT, MODEL_WIDTH)
    out_w = [jnp.concatenate(ring(attention_output_weight[l]), axis=0) for l in range(LAYERS)]
    up_w = [jnp.concatenate(ring(up_weight[l]), axis=1) for l in range(LAYERS)]
    down_w = [jnp.concatenate(ring(down_weight[l]), axis=0) for l in range(LAYERS)]

    frames = features.reshape(slots, CH, FILTER_CHANNELS)
    positions = jnp.arange(CH, dtype=jnp.int32)
    live = (positions[None, :] < block_valid_frames[:, None]).astype(jnp.float32)[:, :, None]
    seen_here = frames_counted[:, None]
    counted = seen_here + block_valid_frames.astype(jnp.float32)[:, None]
    new_mean = (seen_here * feature_running_mean + jnp.sum(live * frames, axis=1)) / counted
    centred = frames - new_mean[:, None, :]
    shifted = feature_running_mean - new_mean
    new_var = (
        seen_here * (feature_running_variance + shifted * shifted)
        + jnp.sum(live * centred * centred, axis=1)
    ) / counted
    normed = (centred / jnp.sqrt(new_var + CMVN_EPS)[:, None, :]).astype(jnp.bfloat16)
    low = jnp.einsum("stm,srm->str", normed, panel_down, preferred_element_type=jnp.float32).astype(
        jnp.bfloat16
    )
    part = dot(normed.reshape(rows, FILTER_CHANNELS), input_weight)
    part = part + jnp.einsum(
        "str,src->stc", low, panel_up, preferred_element_type=jnp.float32
    ).reshape(rows, width)
    state = lax.all_gather(part, "mp", axis=1, tiled=True)

    columns = jnp.arange(FR + CH, dtype=jnp.int32)
    fresh = columns - FR
    allowed = (columns[None, None, :] < FR) | (fresh[None, None, :] <= positions[None, :, None]) & (
        fresh[None, None, :] < block_valid_frames[:, None, None]
    )
    kv_layers = []
    conv_layers = []
    for layer in range(LAYERS):
        attn_in = norm(state, attn_gain[layer])
        qkv = dot(attn_in, query_key_value_weight[layer].reshape(MODEL_WIDTH, -1))
        qkv = qkv.astype(jnp.bfloat16).reshape(slots, CH, 3, heads, HEAD_DIM)
        fresh_kv = jnp.transpose(jnp.concatenate([qkv[:, :, 1], qkv[:, :, 2]], axis=-1), (0, 2, 1, 3))
        both = jnp.concatenate([kv_moved[layer], fresh_kv], axis=2)
        scores = jnp.einsum(
            "bthe,bhse->bhts",
            qkv[:, :, 0],
            both[..., :HEAD_DIM],
            preferred_element_type=jnp.float32,
        ) * HEAD_DIM ** (-0.5)
        scores = jnp.where(allowed[:, None], scores, -1e30)
        peak = jnp.max(scores, axis=-1, keepdims=True)
        weights = jnp.exp(scores - peak)
        probs = (weights / jnp.sum(weights, axis=-1, keepdims=True)).astype(jnp.bfloat16)
        heads_out = jnp.einsum(
            "bhts,bhse->bthe", probs, both[..., HEAD_DIM:], preferred_element_type=jnp.float32
        ).astype(jnp.bfloat16)
        heads_all = jnp.concatenate(ring(heads_out.reshape(rows, width)), axis=1)
        kv_layers.append(
            jnp.transpose(
                window(jnp.transpose(both, (0, 2, 1, 3)), block_valid_frames, FR), (0, 1, 2, 3)
            )
        )
        state = state + dot(heads_all, out_w[layer])
        conv_in = norm(state, conv_gain[layer])
        comb = jnp.concatenate(
            [conv_moved[:, layer], conv_in.reshape(slots, CH, MODEL_WIDTH)], axis=1
        )
        mixed = jnp.zeros((slots, CH, MODEL_WIDTH), jnp.float32)
        for tap in range(KT):
            mixed = mixed + taps[layer, tap] * comb[:, tap : tap + CH].astype(jnp.float32)
        state = state + jax.nn.silu(mixed).reshape(rows, MODEL_WIDTH)
        fresh_conv = lax.dynamic_slice_in_dim(conv_in, mp * width, width, 1)
        own = jnp.concatenate(
            [conv_own[:, layer], fresh_conv.reshape(slots, CH, width)], axis=1
        )
        conv_layers.append(window(own, block_valid_frames, KT - 1))
        ffn_in = norm(state, ffn_gain[layer])
        hidden = jax.nn.silu(dot(ffn_in, up_w[layer])).astype(jnp.bfloat16)
        if layer < LAYERS - 1:
            state = state + dot(hidden, down_w[layer])
    mine_w = lax.dynamic_slice_in_dim(down_w[-1], mp * width, width, 1)
    mine_s = lax.dynamic_slice_in_dim(state, mp * width, width, 1)
    last = mine_s + dot(hidden, mine_w)
    return (
        jnp.transpose(last).astype(jnp.bfloat16),
        jnp.stack(kv_layers, axis=1),
        jnp.stack(conv_layers, axis=1),
        new_mean,
        new_var,
    )


def solution(mesh):
    return jax.shard_map(
        local,
        mesh=mesh,
        in_specs=(
            P("streams", None),
            P("streams"),
            P("streams", None),
            P("streams", None),
            P("streams"),
            P(),
            P(),
            P(),
            P("streams", None, None),
            P("streams", None, "mp"),
            P(None, "mp"),
            P(None, "mp"),
            P(None, None, None, "mp"),
            P(None, "mp", None),
            P(None, "mp"),
            P(None, None, "mp"),
            P(None, "mp"),
            P(None, None, "mp"),
            P(None, "mp", None),
            P("streams", None, None, "mp", None),
            P("streams", None, None, "mp"),
        ),
        out_specs=(
            P("mp", "streams"),
            P("streams", None, None, "mp", None),
            P("streams", None, None, "mp"),
            P("streams", None),
            P("streams", None),
        ),
        check_vma=False,
    )
```

```python
import jax
import jax.numpy as jnp
from jax import lax
from jax.experimental import pallas as pl
from jax.experimental.pallas import tpu as pltpu
from jax.sharding import PartitionSpec as P

MODEL_WIDTH = 768
HEAD_DIM = 64
FILTER_CHANNELS = 80
FR = 64
KT = 31
CH = 16
LAYERS = 2
MP = 4
KV_ROWS = 24
CONV_ROWS = 6
PIECE_ROWS = 32
VMEM_LIMIT = 48 * 1024 * 1024

NORM_EPS = 1e-06
CMVN_EPS = 1e-05


def from_peer(x, shift):
    return lax.ppermute(x, "mp", [((i + shift) % MP, i) for i in range(MP)])


def ring(x):
    return [x] + [from_peer(x, s) for s in range(1, MP)]


def norm(state, gain):
    total = jnp.sum(state * state, axis=-1, keepdims=True)
    spread = jnp.sqrt(total / MODEL_WIDTH + NORM_EPS)
    return (state / spread * gain).astype(jnp.bfloat16)


def dot(a, b):
    return lax.dot_general(a, b, (((1,), (0,)), ((), ())), preferred_element_type=jnp.float32)


def exchange(x):
    return lax.all_to_all(x, "streams", split_axis=0, concat_axis=0, tiled=True)


def peers_in_order(parts):
    first = lax.axis_index("mp")
    order = (jnp.arange(MP, dtype=jnp.int32) - first) % MP
    return jnp.take(jnp.stack(parts), order, axis=0, mode="clip")


def side_by_side(parts):
    ordered = peers_in_order(parts)
    return jnp.concatenate([ordered[c] for c in range(MP)], axis=-1)


def pick_kernel(index, pieces, *outs):
    count = outs[0].shape[0]
    for s, out in enumerate(outs):

        @pl.loop(0, count)
        def _(c, s=s, out=out):
            out[c] = pieces[index[s * count + c], 0]


def pick(index, pieces, layer, planes, count):
    slots, layers, rows, lanes = pieces.shape
    return pl.pallas_call(
        pick_kernel,
        grid=(1,),
        in_specs=[
            pl.BlockSpec(memory_space=pltpu.SMEM),
            pl.BlockSpec((slots, 1, rows, lanes), lambda i: (0, layer, 0, 0)),
        ],
        out_specs=[pl.BlockSpec((count, rows, lanes), lambda i: (0, 0, 0))] * planes,
        out_shape=[jax.ShapeDtypeStruct((count, rows, lanes), pieces.dtype)] * planes,
        compiler_params=pltpu.CompilerParams(vmem_limit_bytes=VMEM_LIMIT),
        name="pick",
    )(index, pieces)


def place_kernel(index, *refs):
    out = refs[-1]
    count = refs[0].shape[0]
    for s, got in enumerate(refs[:-1]):

        @pl.loop(0, count)
        def _(c, s=s, got=got):
            spot = index[s * count + c]

            @pl.when(spot < out.shape[0])
            def _():
                out[spot] = got[c]


def place(index, arrived, slots):
    _, rows, lanes = arrived[0].shape
    return pl.pallas_call(
        place_kernel,
        in_specs=[pl.BlockSpec(memory_space=pltpu.SMEM)]
        + [pl.BlockSpec(memory_space=pltpu.VMEM)] * len(arrived),
        out_specs=pl.BlockSpec(memory_space=pltpu.VMEM),
        out_shape=jax.ShapeDtypeStruct((slots, rows, lanes), arrived[0].dtype),
        compiler_params=pltpu.CompilerParams(vmem_limit_bytes=VMEM_LIMIT),
        name="place",
    )(index, *arrived)


def move_caches(key_value_cache, convolution_cache, slot_relocation):
    slots = key_value_cache.shape[0]
    peers = lax.axis_size("streams")
    me = lax.axis_index("streams")
    group = 8 if peers % 8 == 0 else 2
    planes = peers // group
    plane_slots = group * slots
    room = plane_slots // 4 if planes > 2 else plane_slots // 2
    plane = me // group
    near = [[p * group + j for j in range(group)] for p in range(planes)]

    goes = (slot_relocation // plane_slots).reshape(planes, plane_slots)
    at = jnp.arange(plane_slots, dtype=jnp.int32)
    same = (goes[:, None, :] == goes[:, :, None]) & (at[None, None, :] < at[None, :, None])
    rank = jnp.sum(same.astype(jnp.int32), axis=2)
    fits = jnp.max(rank) < room
    step = jnp.arange(planes, dtype=jnp.int32)
    c = jnp.arange(room, dtype=jnp.int32)
    my_goes = lax.dynamic_index_in_dim(goes, plane, 0, keepdims=False)
    my_rank = lax.dynamic_index_in_dim(rank, plane, 0, keepdims=False)
    match = (my_goes[None, None, :] == ((plane + step) % planes)[:, None, None]) & (
        my_rank[None, None, :] == c[None, :, None]
    )
    out_index = jnp.sum(jnp.where(match, at[None, None, :], 0), axis=2).reshape(-1)
    origin = (plane - step) % planes
    there_goes = jnp.take(goes, origin, axis=0, mode="clip")
    there_rank = jnp.take(rank, origin, axis=0, mode="clip")
    there_spot = jnp.take(
        (slot_relocation % plane_slots).reshape(planes, plane_slots), origin, axis=0, mode="clip"
    )
    match = (there_goes[:, None, :] == plane) & (there_rank[:, None, :] == c[None, :, None])
    in_index = plane_slots + jnp.sum(
        jnp.where(match, there_spot[:, None, :] - plane_slots, 0), axis=2
    ).reshape(-1)

    heads = key_value_cache.shape[3]
    kv = jnp.transpose(key_value_cache, (0, 1, 3, 2, 4)).reshape(
        slots, LAYERS, group, heads * FR // group, 2 * HEAD_DIM
    )
    conv = convolution_cache.reshape(slots, LAYERS, -1, 128)
    conv_rows = -(-conv.shape[2] // group)
    pad = group * conv_rows - conv.shape[2]
    conv = jnp.pad(conv, ((0, 0), (0, 0), (0, pad), (0, 0)))
    conv = conv.reshape(slots, LAYERS, group, conv_rows, 128)
    fill = -(kv.shape[3] + conv_rows) % 16
    conv = jnp.pad(conv, ((0, 0), (0, 0), (0, 0), (0, fill), (0, 0)))
    packed = jnp.concatenate([kv, conv], axis=3)
    rows = packed.shape[3]
    spread = lax.all_to_all(
        jnp.transpose(packed, (2, 0, 1, 3, 4)),
        "streams",
        split_axis=0,
        concat_axis=0,
        axis_index_groups=near,
        tiled=True,
    ).reshape(plane_slots, LAYERS, rows, 128)

    mine = jnp.arange(slots, dtype=jnp.int32)
    peer = jnp.arange(peers, dtype=jnp.int32)

    def dense(layer):
        targets = lax.dynamic_slice_in_dim(slot_relocation, me * slots, slots, 0) // slots
        chosen = jnp.sum(jnp.where(peer[:, None] == targets[None, :], mine[None, :], 0), axis=1)
        anchor = jnp.sum(
            jnp.where(
                slot_relocation[None, :] == (me * slots + mine)[:, None],
                jnp.arange(slot_relocation.shape[0], dtype=jnp.int32)[None, :],
                0,
            ),
            axis=1,
        )
        got = exchange(jnp.take(packed[:, layer], chosen, axis=0, mode="clip"))
        return jnp.take(got, anchor // slots, axis=0, mode="clip")

    moved = []
    for layer in range(LAYERS):
        parts = pick(out_index, spread, layer, planes, room)
        arrived = [parts[0]]
        for s in range(1, planes):
            hop = [
                (p * group + j, (p + s) % planes * group + j)
                for p in range(planes)
                for j in range(group)
            ]
            arrived.append(lax.ppermute(parts[s], "streams", hop))
        here = place(in_index, arrived, plane_slots).reshape(group, slots, rows, 128)
        got = lax.all_to_all(
            here, "streams", split_axis=0, concat_axis=0, axis_index_groups=near, tiled=True
        )
        got = jnp.transpose(got, (1, 0, 2, 3))
        moved.append(lax.cond(fits, lambda x: x, lambda x, l=layer: dense(l), got))
    kv_rows = kv.shape[3]
    kv_moved = [
        m[:, :, :kv_rows].reshape(slots, heads, FR, 2 * HEAD_DIM) for m in moved
    ]
    flat = convolution_cache.shape[2] * convolution_cache.shape[3] // 128
    conv_moved = [
        m[:, :, kv_rows : kv_rows + conv_rows]
        .reshape(slots, group * conv_rows, 128)[:, :flat]
        .reshape((slots,) + convolution_cache.shape[2:])
        for m in moved
    ]
    return kv_moved, conv_moved


def window(frames, block_valid_frames, length):
    picks = block_valid_frames[:, None] + jnp.arange(length, dtype=jnp.int32)[None, :]
    picks = picks.reshape(picks.shape + (1,) * (frames.ndim - 2))
    return jnp.take_along_axis(frames, picks, axis=1)


def local(
    features,
    block_valid_frames,
    feature_running_mean,
    feature_running_variance,
    frames_counted,
    slot_relocation,
    speaker,
    speaker_adapter_row,
    adapter_down_panels,
    adapter_up_panels,
    input_weight,
    attention_norm_gain,
    query_key_value_weight,
    attention_output_weight,
    convolution_norm_gain,
    depthwise_taps,
    feedforward_norm_gain,
    up_weight,
    down_weight,
    key_value_cache,
    convolution_cache,
):
    slots = key_value_cache.shape[0]
    peers = lax.axis_size("streams")
    me = lax.axis_index("streams")
    mp = lax.axis_index("mp")
    first = me * slots
    held = adapter_down_panels.shape[0]
    width = input_weight.shape[1]
    heads = key_value_cache.shape[3]
    rows = slots * CH

    ids = jnp.arange(speaker_adapter_row.shape[0], dtype=jnp.int32)
    all_rows = jnp.sum(
        jnp.where(speaker[:, None] == ids[None, :], speaker_adapter_row[None, :], 0), axis=1
    )
    asked = all_rows.reshape(peers, slots)
    give = jnp.sum(jnp.where(asked // held == me, asked % held, 0), axis=1)
    my_rows = lax.dynamic_slice_in_dim(all_rows, first, slots, 0)
    lanes = 128
    flat_down = adapter_down_panels.reshape(held, -1, lanes)
    flat_up = adapter_up_panels.reshape(held, -1, lanes)
    panels = jnp.concatenate([flat_up, flat_down], axis=1)
    got = exchange(jnp.take(panels, give, axis=0, mode="clip"))
    got = jnp.take(got, my_rows // held, axis=0, mode="clip")
    panel_up = got[:, : flat_up.shape[1]].reshape((slots,) + adapter_up_panels.shape[1:])
    panel_down = got[:, flat_up.shape[1] :].reshape((slots,) + adapter_down_panels.shape[1:])

    kv_moved, conv_own = move_caches(key_value_cache, convolution_cache, slot_relocation)
    conv_moved = [side_by_side(ring(c)) for c in conv_own]

    small = jnp.concatenate(
        [
            attention_norm_gain,
            convolution_norm_gain,
            feedforward_norm_gain,
            depthwise_taps.reshape(LAYERS * KT, width),
        ],
        axis=0,
    )
    small = side_by_side(ring(small))
    attn_gain, conv_gain, ffn_gain = small[0:2], small[2:4], small[4:6]
    taps = small[6:].reshape(LAYERS, KT, MODEL_WIDTH)
    out_w = [jnp.concatenate(ring(attention_output_weight[l]), axis=0) for l in range(LAYERS)]
    up_w = [jnp.concatenate(ring(up_weight[l]), axis=1) for l in range(LAYERS)]
    down_w = [jnp.concatenate(ring(down_weight[l]), axis=0) for l in range(LAYERS)]

    frames = features.reshape(slots, CH, FILTER_CHANNELS)
    positions = jnp.arange(CH, dtype=jnp.int32)
    live = (positions[None, :] < block_valid_frames[:, None]).astype(jnp.float32)[:, :, None]
    seen_here = frames_counted[:, None]
    counted = seen_here + block_valid_frames.astype(jnp.float32)[:, None]
    new_mean = (seen_here * feature_running_mean + jnp.sum(live * frames, axis=1)) / counted
    centred = frames - new_mean[:, None, :]
    shifted = feature_running_mean - new_mean
    new_var = (
        seen_here * (feature_running_variance + shifted * shifted)
        + jnp.sum(live * centred * centred, axis=1)
    ) / counted
    normed = (centred / jnp.sqrt(new_var + CMVN_EPS)[:, None, :]).astype(jnp.bfloat16)
    low = jnp.einsum("stm,srm->str", normed, panel_down, preferred_element_type=jnp.float32).astype(
        jnp.bfloat16
    )
    part = dot(normed.reshape(rows, FILTER_CHANNELS), input_weight)
    part = part + jnp.einsum(
        "str,src->stc", low, panel_up, preferred_element_type=jnp.float32
    ).reshape(rows, width)
    state = side_by_side(ring(part))

    columns = jnp.arange(FR + CH, dtype=jnp.int32)
    fresh = columns - FR
    allowed = (columns[None, None, :] < FR) | (fresh[None, None, :] <= positions[None, :, None]) & (
        fresh[None, None, :] < block_valid_frames[:, None, None]
    )
    kv_layers = []
    conv_layers = []
    for layer in range(LAYERS):
        attn_in = norm(state, attn_gain[layer])
        qkv = dot(attn_in, query_key_value_weight[layer].reshape(MODEL_WIDTH, -1))
        qkv = qkv.astype(jnp.bfloat16).reshape(slots, CH, 3, heads, HEAD_DIM)
        fresh_kv = jnp.transpose(jnp.concatenate([qkv[:, :, 1], qkv[:, :, 2]], axis=-1), (0, 2, 1, 3))
        both = jnp.concatenate([kv_moved[layer], fresh_kv], axis=2)
        scores = jnp.einsum(
            "bthe,bhse->bhts",
            qkv[:, :, 0],
            both[..., :HEAD_DIM],
            preferred_element_type=jnp.float32,
        ) * HEAD_DIM ** (-0.5)
        scores = jnp.where(allowed[:, None], scores, -1e30)
        peak = jnp.max(scores, axis=-1, keepdims=True)
        weights = jnp.exp(scores - peak)
        probs = (weights / jnp.sum(weights, axis=-1, keepdims=True)).astype(jnp.bfloat16)
        heads_out = jnp.einsum(
            "bhts,bhse->bthe", probs, both[..., HEAD_DIM:], preferred_element_type=jnp.float32
        ).astype(jnp.bfloat16)
        heads_all = jnp.concatenate(ring(heads_out.reshape(rows, width)), axis=1)
        kv_layers.append(
            jnp.transpose(
                window(jnp.transpose(both, (0, 2, 1, 3)), block_valid_frames, FR), (0, 1, 2, 3)
            )
        )
        state = state + dot(heads_all, out_w[layer])
        conv_in = norm(state, conv_gain[layer])
        comb = jnp.concatenate(
            [conv_moved[layer], conv_in.reshape(slots, CH, MODEL_WIDTH)], axis=1
        )
        mixed = jnp.zeros((slots, CH, MODEL_WIDTH), jnp.float32)
        for tap in range(KT):
            mixed = mixed + taps[layer, tap] * comb[:, tap : tap + CH].astype(jnp.float32)
        state = state + jax.nn.silu(mixed).reshape(rows, MODEL_WIDTH)
        fresh_conv = lax.dynamic_slice_in_dim(conv_in, mp * width, width, 1)
        own = jnp.concatenate(
            [conv_own[layer], fresh_conv.reshape(slots, CH, width)], axis=1
        )
        conv_layers.append(window(own, block_valid_frames, KT - 1))
        ffn_in = norm(state, ffn_gain[layer])
        hidden = jax.nn.silu(dot(ffn_in, up_w[layer])).astype(jnp.bfloat16)
        if layer < LAYERS - 1:
            state = state + dot(hidden, down_w[layer])
    mine_w = lax.dynamic_slice_in_dim(down_w[-1], mp * width, width, 1)
    mine_s = lax.dynamic_slice_in_dim(state, mp * width, width, 1)
    last = mine_s + dot(hidden, mine_w)
    return (
        jnp.transpose(last).astype(jnp.bfloat16),
        jnp.stack(kv_layers, axis=1),
        jnp.stack(conv_layers, axis=1),
        new_mean,
        new_var,
    )


def solution(mesh):
    return jax.shard_map(
        local,
        mesh=mesh,
        in_specs=(
            P("streams", None),
            P("streams"),
            P("streams", None),
            P("streams", None),
            P("streams"),
            P(),
            P(),
            P(),
            P("streams", None, None),
            P("streams", None, "mp"),
            P(None, "mp"),
            P(None, "mp"),
            P(None, None, None, "mp"),
            P(None, "mp", None),
            P(None, "mp"),
            P(None, None, "mp"),
            P(None, "mp"),
            P(None, None, "mp"),
            P(None, "mp", None),
            P("streams", None, None, "mp", None),
            P("streams", None, None, "mp"),
        ),
        out_specs=(
            P("mp", "streams"),
            P("streams", None, None, "mp", None),
            P("streams", None, None, "mp"),
            P("streams", None),
            P("streams", None),
        ),
        check_vma=False,
    )
```

```python
import functools

import jax
import jax.numpy as jnp
from jax import lax
from jax.experimental import pallas as pl
from jax.experimental.pallas import tpu as pltpu
from jax.sharding import PartitionSpec as P

MODEL_WIDTH = 768
HEAD_DIM = 64
FILTER_CHANNELS = 80
FR = 64
KT = 31
CH = 16
LAYERS = 2
MP = 4
HALF = 32
VMEM_LIMIT = 48 * 1024 * 1024

NORM_EPS = 1e-06
CMVN_EPS = 1e-05


def from_peer(x, shift):
    return lax.ppermute(x, "mp", [((i + shift) % MP, i) for i in range(MP)])


def ring(x):
    return [x] + [from_peer(x, s) for s in range(1, MP)]


def norm(state, gain):
    total = jnp.sum(state * state, axis=-1, keepdims=True)
    spread = jnp.sqrt(total / MODEL_WIDTH + NORM_EPS)
    return (state / spread * gain).astype(jnp.bfloat16)


def dot(a, b):
    return lax.dot_general(a, b, (((1,), (0,)), ((), ())), preferred_element_type=jnp.float32)


def exchange(x):
    return lax.all_to_all(x, "streams", split_axis=0, concat_axis=0, tiled=True)


def peers_in_order(parts):
    first = lax.axis_index("mp")
    order = (jnp.arange(MP, dtype=jnp.int32) - first) % MP
    return jnp.take(jnp.stack(parts), order, axis=0, mode="clip")


def side_by_side(parts):
    ordered = peers_in_order(parts)
    return jnp.concatenate([ordered[c] for c in range(MP)], axis=-1)


def pick_kernel(index, pieces, *outs):
    count = outs[0].shape[0]
    for s, out in enumerate(outs):

        @pl.loop(0, count)
        def _(c, s=s, out=out):
            out[c] = pieces[index[s * count + c], 0]


def pick(index, pieces, layer, planes, count):
    slots, layers, rows, lanes = pieces.shape
    return pl.pallas_call(
        pick_kernel,
        grid=(1,),
        in_specs=[
            pl.BlockSpec(memory_space=pltpu.SMEM),
            pl.BlockSpec((slots, 1, rows, lanes), lambda i: (0, layer, 0, 0)),
        ],
        out_specs=[pl.BlockSpec((count, rows, lanes), lambda i: (0, 0, 0))] * planes,
        out_shape=[jax.ShapeDtypeStruct((count, rows, lanes), pieces.dtype)] * planes,
        compiler_params=pltpu.CompilerParams(vmem_limit_bytes=VMEM_LIMIT),
        name="pick",
    )(index, pieces)


def place_kernel(index, *refs):
    out = refs[-1]
    count = refs[0].shape[0]
    for s, got in enumerate(refs[:-1]):

        @pl.loop(0, count)
        def _(c, s=s, got=got):
            spot = index[s * count + c]

            @pl.when(spot < out.shape[0])
            def _():
                out[spot] = got[c]


def place(index, arrived, slots):
    _, rows, lanes = arrived[0].shape
    return pl.pallas_call(
        place_kernel,
        in_specs=[pl.BlockSpec(memory_space=pltpu.SMEM)]
        + [pl.BlockSpec(memory_space=pltpu.VMEM)] * len(arrived),
        out_specs=pl.BlockSpec(memory_space=pltpu.VMEM),
        out_shape=jax.ShapeDtypeStruct((slots, rows, lanes), arrived[0].dtype),
        compiler_params=pltpu.CompilerParams(vmem_limit_bytes=VMEM_LIMIT),
        name="place",
    )(index, *arrived)


def move_caches(key_value_cache, convolution_cache, slot_relocation):
    slots = key_value_cache.shape[0]
    peers = lax.axis_size("streams")
    me = lax.axis_index("streams")
    group = 8 if peers % 8 == 0 else 2
    planes = peers // group
    plane_slots = group * slots
    room = plane_slots // 4 if planes > 2 else plane_slots // 2
    plane = me // group
    near = [[p * group + j for j in range(group)] for p in range(planes)]

    goes = (slot_relocation // plane_slots).reshape(planes, plane_slots)
    at = jnp.arange(plane_slots, dtype=jnp.int32)
    same = (goes[:, None, :] == goes[:, :, None]) & (at[None, None, :] < at[None, :, None])
    rank = jnp.sum(same.astype(jnp.int32), axis=2)
    fits = jnp.max(rank) < room
    step = jnp.arange(planes, dtype=jnp.int32)
    c = jnp.arange(room, dtype=jnp.int32)
    my_goes = lax.dynamic_index_in_dim(goes, plane, 0, keepdims=False)
    my_rank = lax.dynamic_index_in_dim(rank, plane, 0, keepdims=False)
    match = (my_goes[None, None, :] == ((plane + step) % planes)[:, None, None]) & (
        my_rank[None, None, :] == c[None, :, None]
    )
    out_index = jnp.sum(jnp.where(match, at[None, None, :], 0), axis=2).reshape(-1)
    origin = (plane - step) % planes
    there_goes = jnp.take(goes, origin, axis=0, mode="clip")
    there_rank = jnp.take(rank, origin, axis=0, mode="clip")
    there_spot = jnp.take(
        (slot_relocation % plane_slots).reshape(planes, plane_slots), origin, axis=0, mode="clip"
    )
    match = (there_goes[:, None, :] == plane) & (there_rank[:, None, :] == c[None, :, None])
    in_index = plane_slots + jnp.sum(
        jnp.where(match, there_spot[:, None, :] - plane_slots, 0), axis=2
    ).reshape(-1)

    heads = key_value_cache.shape[3]
    kv = jnp.transpose(key_value_cache, (0, 1, 3, 2, 4)).reshape(
        slots, LAYERS, group, heads * FR // group, 2 * HEAD_DIM
    )
    taken = convolution_cache.shape[2]
    low = jnp.pad(convolution_cache[..., :128], ((0, 0), (0, 0), (0, HALF - taken), (0, 0)))
    high = jnp.pad(
        convolution_cache[..., 128:],
        ((0, 0), (0, 0), (0, HALF - taken), (0, 256 - convolution_cache.shape[3])),
    )
    conv = jnp.concatenate([low, high], axis=2).reshape(
        slots, LAYERS, group, 2 * HALF // group, 128
    )
    packed = jnp.concatenate([kv, conv], axis=3)
    rows = packed.shape[3]
    spread = lax.all_to_all(
        jnp.transpose(packed, (2, 0, 1, 3, 4)),
        "streams",
        split_axis=0,
        concat_axis=0,
        axis_index_groups=near,
        tiled=True,
    ).reshape(plane_slots, LAYERS, rows, 128)

    mine = jnp.arange(slots, dtype=jnp.int32)
    peer = jnp.arange(peers, dtype=jnp.int32)

    def dense(layer):
        targets = lax.dynamic_slice_in_dim(slot_relocation, me * slots, slots, 0) // slots
        chosen = jnp.sum(jnp.where(peer[:, None] == targets[None, :], mine[None, :], 0), axis=1)
        anchor = jnp.sum(
            jnp.where(
                slot_relocation[None, :] == (me * slots + mine)[:, None],
                jnp.arange(slot_relocation.shape[0], dtype=jnp.int32)[None, :],
                0,
            ),
            axis=1,
        )
        got = exchange(jnp.take(packed[:, layer], chosen, axis=0, mode="clip"))
        return jnp.transpose(jnp.take(got, anchor // slots, axis=0, mode="clip"), (1, 0, 2, 3))

    moved = []
    for layer in range(LAYERS):
        parts = pick(out_index, spread, layer, planes, room)
        arrived = [parts[0]]
        for s in range(1, planes):
            hop = [
                (p * group + j, (p + s) % planes * group + j)
                for p in range(planes)
                for j in range(group)
            ]
            arrived.append(lax.ppermute(parts[s], "streams", hop))
        here = place(in_index, arrived, plane_slots).reshape(group, slots, rows, 128)
        got = lax.all_to_all(
            here, "streams", split_axis=0, concat_axis=0, axis_index_groups=near, tiled=True
        )
        moved.append(lax.cond(fits, lambda x: x, lambda x, l=layer: dense(l), got))
    kv_rows = kv.shape[3]
    conv_moved = []
    for m in moved:
        c = jnp.transpose(m[:, :, kv_rows:], (0, 2, 1, 3)).reshape(2, HALF, slots, 128)
        conv_moved.append(
            jnp.concatenate(
                [c[0, :taken], c[1, :taken, :, : convolution_cache.shape[3] - 128]], axis=-1
            )
        )
    return moved, conv_moved, spread


def attention_kernel(valid, order, bias, qkv, got, *rest):
    heads_out, kv_out, both, sorted_rows, packed = rest[-5:]
    group, slots, rows, lanes = got.shape
    heads = both.shape[1]
    kv_rows = heads * FR // group

    sorted_rows[...] = jnp.dot(
        order[...], qkv[...], preferred_element_type=jnp.float32
    ).astype(jnp.bfloat16)

    @pl.loop(0, slots)
    def _(s):
        for p in range(group):
            piece = got[p, s].astype(jnp.float32)
            for r in range(0, kv_rows, 8):
                q = p * kv_rows + r
                both[s, q // FR, q % FR : q % FR + 8, :] = piece[r : r + 8]
        new = sorted_rows[pl.ds(pl.multiple_of(s * CH, CH), CH), heads * lanes :]
        for h in range(heads):
            both[s, h, FR:, :] = new[:, h * lanes : (h + 1) * lanes].astype(jnp.float32)
            kv_out[s, 0, h] = both[s, h, pl.ds(valid[s], FR), :].astype(jnp.bfloat16)

    step = 4
    span = step * CH
    lane = lax.broadcasted_iota(jnp.int32, (span, lanes), 1)
    for g in range(slots // step):
        part = slice(g * span, (g + 1) * span)
        outs = []
        for h in range(heads):
            keys = both[g * step : (g + 1) * step, h].reshape(step * (FR + CH), lanes)
            keys = keys.astype(jnp.bfloat16)
            q = sorted_rows[part, h * lanes : (h + 1) * lanes]
            scores = lax.dot_general(
                q, keys, (((1,), (1,)), ((), ())), preferred_element_type=jnp.float32
            )
            scores = scores * HEAD_DIM ** (-0.5) + bias[part, :]
            peak = jnp.max(scores, axis=-1, keepdims=True)
            weights = jnp.exp(scores - peak)
            probs = (weights / jnp.sum(weights, axis=-1, keepdims=True)).astype(jnp.bfloat16)
            outs.append(jnp.dot(probs, keys, preferred_element_type=jnp.float32))
        first = jnp.where(lane < HEAD_DIM, pltpu.roll(outs[0], HEAD_DIM, 1), outs[1])
        second = pltpu.roll(outs[2], HEAD_DIM, 1)
        packed[part, :] = jnp.concatenate([first, second], axis=1).astype(jnp.bfloat16)
    back = lax.dot_general(
        order[...], packed[...], (((0,), (0,)), ((), ())), preferred_element_type=jnp.float32
    )
    heads_out[...] = back[:, : heads_out.shape[1]].astype(jnp.bfloat16)


def attention(layer, valid, order, bias, qkv, got, kv_so_far, heads):
    group, slots, rows, lanes = got.shape
    frames = qkv.shape[0]
    vmem = pl.BlockSpec(memory_space=pltpu.VMEM)
    more = [] if kv_so_far is None else [kv_so_far]
    return pl.pallas_call(
        attention_kernel,
        grid=(1,),
        in_specs=[pl.BlockSpec(memory_space=pltpu.SMEM)]
        + [vmem] * 4
        + [pl.BlockSpec(memory_space=pl.ANY)] * len(more),
        out_specs=[
            vmem,
            pl.BlockSpec((slots, 1, heads, FR, lanes), lambda i: (0, layer, 0, 0, 0)),
        ],
        out_shape=[
            jax.ShapeDtypeStruct((frames, heads * HEAD_DIM), jnp.bfloat16),
            jax.ShapeDtypeStruct((slots, LAYERS, heads, FR, lanes), jnp.bfloat16),
        ],
        scratch_shapes=[
            pltpu.VMEM((slots, heads, FR + CH, lanes), jnp.float32),
            pltpu.VMEM(qkv.shape, jnp.bfloat16),
            pltpu.VMEM((frames, 2 * lanes), jnp.bfloat16),
        ],
        input_output_aliases={5: 1} if more else {},
        compiler_params=pltpu.CompilerParams(vmem_limit_bytes=VMEM_LIMIT),
        name="attention",
    )(valid, order, bias, qkv, got, *more)


def silu(v):
    return v / (1.0 + jnp.exp(-v))


def block_kernel(last, place_of, state_in, valid, conv_gain, ffn_gain, next_gain, taps, cache, *rest):
    heads, out_w = rest[0:MP], rest[MP : 2 * MP]
    up_w, down_w = rest[2 * MP : 3 * MP], rest[3 * MP : 4 * MP]
    tail, rest = rest[4 * MP], rest[4 * MP + 1 :]
    if last:
        result, new_conv, state, comb, own = rest
    else:
        state_out, result, new_conv, state, comb, own = rest
    frames, width = state_in.shape
    slots = frames // CH
    share = new_conv.shape[2]
    kept = KT - 1

    total = state_in[...]
    for h, w in zip(heads, out_w):
        total = total + jnp.dot(h[...], w[...], preferred_element_type=jnp.float32)
    state[...] = total
    conv_in = norm(total, conv_gain[...])
    comb[kept:] = conv_in.astype(jnp.float32).reshape(CH, slots, width)
    comb[:kept] = cache[...].astype(jnp.float32)

    @pl.loop(0, width // 128)
    def _(c):
        lanes = pl.ds(pl.multiple_of(c * 128, 128), 128)
        for t in range(CH):
            mixed = taps[0:1, lanes] * comb[t, :, lanes]
            for k in range(1, KT):
                mixed = mixed + taps[k : k + 1, lanes] * comb[t + k, :, lanes]
            where = slice(t * slots, (t + 1) * slots)
            state[where, lanes] = state[where, lanes] + silu(mixed)

    for m in range(MP):

        @pl.when(place_of[0] == m)
        def _(m=m):
            own[...] = comb[:, :, m * share : (m + 1) * share]

    masks = [jnp.broadcast_to(valid[...] == v, (slots, share)) for v in range(1, CH + 1)]
    for j in range(kept):
        picked = own[j + 1]
        for v in range(2, CH + 1):
            picked = jnp.where(masks[v - 1], own[j + v], picked)
        new_conv[j] = picked.astype(jnp.bfloat16)

    total = state[...]
    ffn_in = norm(total, ffn_gain[...])
    for u, d in zip(up_w, down_w):
        hidden = silu(jnp.dot(ffn_in, u[...], preferred_element_type=jnp.float32))
        total = total + jnp.dot(
            hidden.astype(jnp.bfloat16), d[...], preferred_element_type=jnp.float32
        )
    if last:
        rounded = total.astype(jnp.bfloat16)
        for m in range(MP):

            @pl.when(place_of[0] == m)
            def _(m=m):
                result[...] = lax.dot_general(
                    rounded[:, m * share : (m + 1) * share],
                    tail[...],
                    (((0,), (1,)), ((), ())),
                    preferred_element_type=jnp.float32,
                ).astype(jnp.bfloat16)

    else:
        state_out[...] = total
        result[...] = lax.dot_general(
            norm(total, next_gain[...]),
            tail[...],
            (((1,), (1,)), ((), ())),
            preferred_element_type=jnp.float32,
        ).astype(jnp.bfloat16)


def block(last, state, valid, gains, taps, cache, heads, out_w, up_w, down_w, tail, share):
    frames, width = state.shape
    slots = frames // CH
    vmem = pl.BlockSpec(memory_space=pltpu.VMEM)
    place_of = lax.axis_index("mp").reshape(1)
    args = [state, valid, *gains, taps, cache, *heads, *out_w, *up_w, *down_w, tail]
    conv_shape = jax.ShapeDtypeStruct((KT - 1, slots, share), jnp.bfloat16)
    if last:
        shapes = [jax.ShapeDtypeStruct((share, frames), jnp.bfloat16), conv_shape]
    else:
        shapes = [
            jax.ShapeDtypeStruct((frames, width), jnp.float32),
            jax.ShapeDtypeStruct((frames, tail.shape[0]), jnp.bfloat16),
            conv_shape,
        ]
    return pl.pallas_call(
        functools.partial(block_kernel, last),
        in_specs=[pl.BlockSpec(memory_space=pltpu.SMEM)] + [vmem] * len(args),
        out_specs=[vmem] * len(shapes),
        out_shape=shapes,
        scratch_shapes=[
            pltpu.VMEM((frames, width), jnp.float32),
            pltpu.VMEM((KT - 1 + CH, slots, width), jnp.float32),
            pltpu.VMEM((KT - 1 + CH, slots, share), jnp.float32),
        ],
        compiler_params=pltpu.CompilerParams(vmem_limit_bytes=VMEM_LIMIT),
        name="block",
    )(place_of, *args)


def local(
    features,
    block_valid_frames,
    feature_running_mean,
    feature_running_variance,
    frames_counted,
    slot_relocation,
    speaker,
    speaker_adapter_row,
    adapter_down_panels,
    adapter_up_panels,
    input_weight,
    attention_norm_gain,
    query_key_value_weight,
    attention_output_weight,
    convolution_norm_gain,
    depthwise_taps,
    feedforward_norm_gain,
    up_weight,
    down_weight,
    key_value_cache,
    convolution_cache,
):
    slots = key_value_cache.shape[0]
    peers = lax.axis_size("streams")
    me = lax.axis_index("streams")
    mp = lax.axis_index("mp")
    first = me * slots
    held = adapter_down_panels.shape[0]
    width = input_weight.shape[1]
    heads = key_value_cache.shape[3]
    rows = slots * CH

    moved, conv_own, spread = move_caches(key_value_cache, convolution_cache, slot_relocation)

    small = jnp.concatenate(
        [
            attention_norm_gain,
            convolution_norm_gain,
            feedforward_norm_gain,
            depthwise_taps.reshape(LAYERS * KT, width),
        ],
        axis=0,
    )
    small = side_by_side(ring(small))
    attn_gain, conv_gain, ffn_gain = small[0:2], small[2:4], small[4:6]
    taps = small[6:].reshape(LAYERS, KT, MODEL_WIDTH)
    out_w = [ring(attention_output_weight[l]) for l in range(LAYERS)]
    up_w = [ring(up_weight[l]) for l in range(LAYERS)]
    down_w = [ring(down_weight[l]) for l in range(LAYERS)]
    qkv_w = []
    for l in range(LAYERS):
        w = jnp.transpose(query_key_value_weight[l], (1, 2, 0))
        w = w.reshape(3, heads, HEAD_DIM, MODEL_WIDTH)
        pairs = jnp.stack(
            [
                jnp.stack([w[0], jnp.zeros_like(w[0])], axis=1),
                jnp.stack([w[1], w[2]], axis=1),
            ]
        )
        qkv_w.append(pairs.reshape(4 * heads * HEAD_DIM, MODEL_WIDTH))

    ids = jnp.arange(speaker_adapter_row.shape[0], dtype=jnp.int32)
    all_rows = jnp.sum(
        jnp.where(speaker[:, None] == ids[None, :], speaker_adapter_row[None, :], 0), axis=1
    )
    asked = all_rows.reshape(peers, slots)
    give = jnp.sum(jnp.where(asked // held == me, asked % held, 0), axis=1)
    my_rows = lax.dynamic_slice_in_dim(all_rows, first, slots, 0)
    flat_down = adapter_down_panels.reshape(held, -1, 128)
    flat_up = adapter_up_panels.reshape(held, -1, 128)
    panels = jnp.concatenate([flat_up, flat_down], axis=1)
    panels = jnp.take(panels, give, axis=0, mode="clip")
    panels, _ = lax.optimization_barrier((panels, spread))
    got = exchange(panels)
    got = jnp.take(got, my_rows // held, axis=0, mode="clip")
    panel_up = got[:, : flat_up.shape[1]].reshape((slots,) + adapter_up_panels.shape[1:])
    panel_down = got[:, flat_up.shape[1] :].reshape((slots,) + adapter_down_panels.shape[1:])

    frames = features.reshape(slots, CH, FILTER_CHANNELS)
    positions = jnp.arange(CH, dtype=jnp.int32)
    live = (positions[None, :] < block_valid_frames[:, None]).astype(jnp.float32)[:, :, None]
    seen_here = frames_counted[:, None]
    counted = seen_here + block_valid_frames.astype(jnp.float32)[:, None]
    new_mean = (seen_here * feature_running_mean + jnp.sum(live * frames, axis=1)) / counted
    centred = frames - new_mean[:, None, :]
    shifted = feature_running_mean - new_mean
    new_var = (
        seen_here * (feature_running_variance + shifted * shifted)
        + jnp.sum(live * centred * centred, axis=1)
    ) / counted
    normed = (centred / jnp.sqrt(new_var + CMVN_EPS)[:, None, :]).astype(jnp.bfloat16)
    low = jnp.einsum("stm,srm->str", normed, panel_down, preferred_element_type=jnp.float32).astype(
        jnp.bfloat16
    )
    part = dot(normed.reshape(rows, FILTER_CHANNELS), input_weight)
    part = part + jnp.einsum(
        "str,src->stc", low, panel_up, preferred_element_type=jnp.float32
    ).reshape(rows, width)
    part = jnp.transpose(part.reshape(slots, CH, width), (1, 0, 2)).reshape(rows, width)
    state = side_by_side(ring(part))

    row = jnp.arange(rows, dtype=jnp.int32)
    row_slot, row_frame = row // CH, row % CH
    order = (row[None, :] == (row_frame * slots + row_slot)[:, None]).astype(jnp.bfloat16)
    column = jnp.arange(4 * (FR + CH), dtype=jnp.int32)
    fresh = (column % (FR + CH) - FR)[None, :]
    allowed = (row_slot % 4)[:, None] == (column // (FR + CH))[None, :]
    row_valid = jnp.repeat(block_valid_frames, CH)[:, None]
    allowed = allowed & ((fresh < 0) | (fresh <= row_frame[:, None]) & (fresh < row_valid))
    bias = jnp.where(allowed, 0.0, -1e30).astype(jnp.float32)
    valid = block_valid_frames[:, None]

    qkv = lax.dot_general(
        norm(state, attn_gain[0]),
        qkv_w[0],
        (((1,), (1,)), ((), ())),
        preferred_element_type=jnp.float32,
    ).astype(jnp.bfloat16)
    kv_out = None
    conv_out = []
    for layer in range(LAYERS):
        last = layer == LAYERS - 1
        held_w = (out_w[layer], up_w[layer], down_w[layer])
        got, held_w = lax.optimization_barrier((moved[layer], held_w))
        heads_out, kv_out = attention(
            layer, block_valid_frames, order, bias, qkv, got, kv_out, heads
        )
        cache = side_by_side(ring(conv_own[layer]))
        following = 0 if last else layer + 1
        gains = [
            conv_gain[layer : layer + 1],
            ffn_gain[layer : layer + 1],
            attn_gain[following : following + 1],
        ]
        done = block(
            last,
            state,
            valid,
            gains,
            taps[layer],
            cache,
            ring(heads_out),
            *held_w,
            order if last else qkv_w[layer + 1],
            width,
        )
        conv_out.append(done[-1])
        if last:
            enc_out = done[0]
        else:
            state, qkv = done[0], done[1]
    return (
        enc_out,
        jnp.transpose(kv_out, (0, 1, 3, 2, 4)),
        jnp.transpose(jnp.stack(conv_out), (2, 0, 1, 3)),
        new_mean,
        new_var,
    )


def solution(mesh):
    return jax.shard_map(
        local,
        mesh=mesh,
        in_specs=(
            P("streams", None),
            P("streams"),
            P("streams", None),
            P("streams", None),
            P("streams"),
            P(),
            P(),
            P(),
            P("streams", None, None),
            P("streams", None, "mp"),
            P(None, "mp"),
            P(None, "mp"),
            P(None, None, None, "mp"),
            P(None, "mp", None),
            P(None, "mp"),
            P(None, None, "mp"),
            P(None, "mp"),
            P(None, None, "mp"),
            P(None, "mp", None),
            P("streams", None, None, "mp", None),
            P("streams", None, None, "mp"),
        ),
        out_specs=(
            P("mp", "streams"),
            P("streams", None, None, "mp", None),
            P("streams", None, None, "mp"),
            P("streams", None),
            P("streams", None),
        ),
        check_vma=False,
    )
```

```python
import functools

import jax
import jax.numpy as jnp
from jax import lax
from jax.experimental import pallas as pl
from jax.experimental.pallas import tpu as pltpu
from jax.sharding import PartitionSpec as P

MODEL_WIDTH = 768
HEAD_DIM = 64
FILTER_CHANNELS = 80
FR = 64
KT = 31
CH = 16
LAYERS = 2
MP = 4
HALF = 32
VMEM_LIMIT = 48 * 1024 * 1024

NORM_EPS = 1e-06
CMVN_EPS = 1e-05


def from_peer(x, shift):
    return lax.ppermute(x, "mp", [((i + shift) % MP, i) for i in range(MP)])


def ring(x):
    return [x] + [from_peer(x, s) for s in range(1, MP)]


def norm(state, gain):
    total = jnp.sum(state * state, axis=-1, keepdims=True)
    spread = jnp.sqrt(total / MODEL_WIDTH + NORM_EPS)
    return (state / spread * gain).astype(jnp.bfloat16)


def dot(a, b):
    return lax.dot_general(a, b, (((1,), (0,)), ((), ())), preferred_element_type=jnp.float32)


def exchange(x):
    return lax.all_to_all(x, "streams", split_axis=0, concat_axis=0, tiled=True)


def peers_in_order(parts):
    first = lax.axis_index("mp")
    order = (jnp.arange(MP, dtype=jnp.int32) - first) % MP
    return jnp.take(jnp.stack(parts), order, axis=0, mode="clip")


def side_by_side(parts):
    ordered = peers_in_order(parts)
    return jnp.concatenate([ordered[c] for c in range(MP)], axis=-1)


def pick_kernel(index, pieces, *outs):
    count = outs[0].shape[0]
    for s, out in enumerate(outs):

        @pl.loop(0, count)
        def _(c, s=s, out=out):
            out[c] = pieces[index[s * count + c], 0]


def pick(index, pieces, layer, planes, count):
    slots, layers, rows, lanes = pieces.shape
    return pl.pallas_call(
        pick_kernel,
        grid=(1,),
        in_specs=[
            pl.BlockSpec(memory_space=pltpu.SMEM),
            pl.BlockSpec((slots, 1, rows, lanes), lambda i: (0, layer, 0, 0)),
        ],
        out_specs=[pl.BlockSpec((count, rows, lanes), lambda i: (0, 0, 0))] * planes,
        out_shape=[jax.ShapeDtypeStruct((count, rows, lanes), pieces.dtype)] * planes,
        compiler_params=pltpu.CompilerParams(vmem_limit_bytes=VMEM_LIMIT),
        name="pick",
    )(index, pieces)


def place_kernel(index, *refs):
    out = refs[-1]
    count = refs[0].shape[0]
    for s, got in enumerate(refs[:-1]):

        @pl.loop(0, count)
        def _(c, s=s, got=got):
            spot = index[s * count + c]

            @pl.when(spot < out.shape[0])
            def _():
                out[spot] = got[c]


def place(index, arrived, slots):
    _, rows, lanes = arrived[0].shape
    return pl.pallas_call(
        place_kernel,
        in_specs=[pl.BlockSpec(memory_space=pltpu.SMEM)]
        + [pl.BlockSpec(memory_space=pltpu.VMEM)] * len(arrived),
        out_specs=pl.BlockSpec(memory_space=pltpu.VMEM),
        out_shape=jax.ShapeDtypeStruct((slots, rows, lanes), arrived[0].dtype),
        compiler_params=pltpu.CompilerParams(vmem_limit_bytes=VMEM_LIMIT),
        name="place",
    )(index, *arrived)


def move_caches(key_value_cache, convolution_cache, slot_relocation):
    slots = key_value_cache.shape[0]
    peers = lax.axis_size("streams")
    me = lax.axis_index("streams")
    group = 8 if peers % 8 == 0 else 2
    planes = peers // group
    plane_slots = group * slots
    room = plane_slots // 4 if planes > 2 else plane_slots // 2
    plane = me // group
    near = [[p * group + j for j in range(group)] for p in range(planes)]

    goes = (slot_relocation // plane_slots).reshape(planes, plane_slots)
    at = jnp.arange(plane_slots, dtype=jnp.int32)
    same = (goes[:, None, :] == goes[:, :, None]) & (at[None, None, :] < at[None, :, None])
    rank = jnp.sum(same.astype(jnp.int32), axis=2)
    fits = jnp.max(rank) < room
    step = jnp.arange(planes, dtype=jnp.int32)
    c = jnp.arange(room, dtype=jnp.int32)
    my_goes = lax.dynamic_index_in_dim(goes, plane, 0, keepdims=False)
    my_rank = lax.dynamic_index_in_dim(rank, plane, 0, keepdims=False)
    match = (my_goes[None, None, :] == ((plane + step) % planes)[:, None, None]) & (
        my_rank[None, None, :] == c[None, :, None]
    )
    out_index = jnp.sum(jnp.where(match, at[None, None, :], 0), axis=2).reshape(-1)
    origin = (plane - step) % planes
    there_goes = jnp.take(goes, origin, axis=0, mode="clip")
    there_rank = jnp.take(rank, origin, axis=0, mode="clip")
    there_spot = jnp.take(
        (slot_relocation % plane_slots).reshape(planes, plane_slots), origin, axis=0, mode="clip"
    )
    match = (there_goes[:, None, :] == plane) & (there_rank[:, None, :] == c[None, :, None])
    in_index = plane_slots + jnp.sum(
        jnp.where(match, there_spot[:, None, :] - plane_slots, 0), axis=2
    ).reshape(-1)

    heads = key_value_cache.shape[3]
    kv = jnp.transpose(key_value_cache, (0, 1, 3, 2, 4)).reshape(
        slots, LAYERS, group, heads * FR // group, 2 * HEAD_DIM
    )
    taken = convolution_cache.shape[2]
    low = jnp.pad(convolution_cache[..., :128], ((0, 0), (0, 0), (0, HALF - taken), (0, 0)))
    high = jnp.pad(
        convolution_cache[..., 128:],
        ((0, 0), (0, 0), (0, HALF - taken), (0, 256 - convolution_cache.shape[3])),
    )
    conv = jnp.concatenate([low, high], axis=2).reshape(
        slots, LAYERS, group, 2 * HALF // group, 128
    )
    packed = jnp.concatenate([kv, conv], axis=3)
    rows = packed.shape[3]
    spread = lax.all_to_all(
        jnp.transpose(packed, (2, 0, 1, 3, 4)),
        "streams",
        split_axis=0,
        concat_axis=0,
        axis_index_groups=near,
        tiled=True,
    ).reshape(plane_slots, LAYERS, rows, 128)

    mine = jnp.arange(slots, dtype=jnp.int32)
    peer = jnp.arange(peers, dtype=jnp.int32)

    def dense(layer):
        targets = lax.dynamic_slice_in_dim(slot_relocation, me * slots, slots, 0) // slots
        chosen = jnp.sum(jnp.where(peer[:, None] == targets[None, :], mine[None, :], 0), axis=1)
        anchor = jnp.sum(
            jnp.where(
                slot_relocation[None, :] == (me * slots + mine)[:, None],
                jnp.arange(slot_relocation.shape[0], dtype=jnp.int32)[None, :],
                0,
            ),
            axis=1,
        )
        got = exchange(jnp.take(packed[:, layer], chosen, axis=0, mode="clip"))
        return jnp.transpose(jnp.take(got, anchor // slots, axis=0, mode="clip"), (1, 0, 2, 3))

    kv_rows = kv.shape[3]

    def begin_by_steps(layer, pieces):
        parts = pick(out_index, pieces, layer, planes, room)
        arrived = [parts[0]]
        for s in range(1, planes):
            hop = [
                (p * group + j, (p + s) % planes * group + j)
                for p in range(planes)
                for j in range(group)
            ]
            arrived.append(lax.ppermute(parts[s], "streams", hop))
        return arrived

    def pick_in_order(layer, pieces):
        index = jnp.take(out_index.reshape(planes, room), (step - plane) % planes, axis=0, mode="clip")
        return pick(index.reshape(-1), pieces, layer, 1, planes * room)[0]

    def begin_at_once(part):
        far = [[p * group + j for p in range(planes)] for j in range(group)]
        return lax.all_to_all(
            part, "streams", split_axis=0, concat_axis=0, axis_index_groups=far, tiled=True
        )

    def finish(arrived):
        index = in_index
        if not isinstance(arrived, list):
            index = jnp.take(index.reshape(planes, room), (plane - step) % planes, axis=0, mode="clip")
            index, arrived = index.reshape(-1), [arrived]
        here = place(index, arrived, plane_slots).reshape(group, slots, rows, 128)
        return lax.all_to_all(
            here, "streams", split_axis=0, concat_axis=0, axis_index_groups=near, tiled=True
        )

    def settle(layer, got):
        got = lax.cond(fits, lambda x: x, lambda x: dense(layer), got)
        c = jnp.transpose(got[:, :, kv_rows:], (0, 2, 1, 3)).reshape(2, HALF, slots, 128)
        own = jnp.concatenate(
            [c[0, :taken], c[1, :taken, :, : convolution_cache.shape[3] - 128]], axis=-1
        )
        return got, own

    return spread, begin_by_steps, pick_in_order, begin_at_once, finish, settle


def attention_kernel(valid, order, bias, qkv, got, *rest):
    heads_out, kv_out, both, sorted_rows, packed = rest[-5:]
    group, slots, rows, lanes = got.shape
    heads = both.shape[1]
    kv_rows = heads * FR // group

    sorted_rows[...] = jnp.dot(
        order[...], qkv[...], preferred_element_type=jnp.float32
    ).astype(jnp.bfloat16)

    @pl.loop(0, slots)
    def _(s):
        for p in range(group):
            piece = got[p, s].astype(jnp.float32)
            for r in range(0, kv_rows, 8):
                q = p * kv_rows + r
                both[s, q // FR, q % FR : q % FR + 8, :] = piece[r : r + 8]
        new = sorted_rows[pl.ds(pl.multiple_of(s * CH, CH), CH), heads * lanes :]
        for h in range(heads):
            both[s, h, FR:, :] = new[:, h * lanes : (h + 1) * lanes].astype(jnp.float32)
            kv_out[s, 0, h] = both[s, h, pl.ds(valid[s], FR), :].astype(jnp.bfloat16)

    step = 4
    span = step * CH
    lane = lax.broadcasted_iota(jnp.int32, (span, lanes), 1)
    for g in range(slots // step):
        part = slice(g * span, (g + 1) * span)
        outs = []
        for h in range(heads):
            keys = both[g * step : (g + 1) * step, h].reshape(step * (FR + CH), lanes)
            keys = keys.astype(jnp.bfloat16)
            q = sorted_rows[part, h * lanes : (h + 1) * lanes]
            scores = lax.dot_general(
                q, keys, (((1,), (1,)), ((), ())), preferred_element_type=jnp.float32
            )
            scores = scores * HEAD_DIM ** (-0.5) + bias[part, :]
            peak = jnp.max(scores, axis=-1, keepdims=True)
            weights = jnp.exp(scores - peak)
            probs = (weights / jnp.sum(weights, axis=-1, keepdims=True)).astype(jnp.bfloat16)
            outs.append(jnp.dot(probs, keys, preferred_element_type=jnp.float32))
        first = jnp.where(lane < HEAD_DIM, pltpu.roll(outs[0], HEAD_DIM, 1), outs[1])
        second = pltpu.roll(outs[2], HEAD_DIM, 1)
        packed[part, :] = jnp.concatenate([first, second], axis=1).astype(jnp.bfloat16)
    back = lax.dot_general(
        order[...], packed[...], (((0,), (0,)), ((), ())), preferred_element_type=jnp.float32
    )
    heads_out[...] = back[:, : heads_out.shape[1]].astype(jnp.bfloat16)


def attention(layer, valid, order, bias, qkv, got, kv_so_far, heads):
    group, slots, rows, lanes = got.shape
    frames = qkv.shape[0]
    vmem = pl.BlockSpec(memory_space=pltpu.VMEM)
    more = [] if kv_so_far is None else [kv_so_far]
    return pl.pallas_call(
        attention_kernel,
        grid=(1,),
        in_specs=[pl.BlockSpec(memory_space=pltpu.SMEM)]
        + [vmem] * 4
        + [pl.BlockSpec(memory_space=pl.ANY)] * len(more),
        out_specs=[
            vmem,
            pl.BlockSpec((slots, 1, heads, FR, lanes), lambda i: (0, layer, 0, 0, 0)),
        ],
        out_shape=[
            jax.ShapeDtypeStruct((frames, heads * HEAD_DIM), jnp.bfloat16),
            jax.ShapeDtypeStruct((slots, LAYERS, heads, FR, lanes), jnp.bfloat16),
        ],
        scratch_shapes=[
            pltpu.VMEM((slots, heads, FR + CH, lanes), jnp.float32),
            pltpu.VMEM(qkv.shape, jnp.bfloat16),
            pltpu.VMEM((frames, 2 * lanes), jnp.bfloat16),
        ],
        input_output_aliases={5: 1} if more else {},
        compiler_params=pltpu.CompilerParams(vmem_limit_bytes=VMEM_LIMIT),
        name="attention",
    )(valid, order, bias, qkv, got, *more)


def silu(v):
    return v / (1.0 + jnp.exp(-v))


def block_kernel(last, place_of, state_in, valid, conv_gain, ffn_gain, next_gain, taps, cache, *rest):
    heads, (weights, tail), rest = rest[0:MP], rest[MP : MP + 2], rest[MP + 2 :]
    if last:
        result, new_conv, state, comb, own = rest
    else:
        state_out, result, new_conv, state, comb, own = rest
    frames, width = state_in.shape
    slots = frames // CH
    share = new_conv.shape[2]
    kept = KT - 1

    hidden_units = (weights.shape[1] - share) // 2
    total = state_in[...]
    for s, h in enumerate(heads):
        w = weights[(place_of[0] + s) % MP, :share, :]
        total = total + jnp.dot(h[...], w, preferred_element_type=jnp.float32)
    state[...] = total
    conv_in = norm(total, conv_gain[...])
    comb[kept:] = conv_in.astype(jnp.float32).reshape(CH, slots, width)
    comb[:kept] = cache[...].astype(jnp.float32)

    @pl.loop(0, width // 128)
    def _(c):
        lanes = pl.ds(pl.multiple_of(c * 128, 128), 128)
        for t in range(CH):
            mixed = taps[0:1, lanes] * comb[t, :, lanes]
            for k in range(1, KT):
                mixed = mixed + taps[k : k + 1, lanes] * comb[t + k, :, lanes]
            where = slice(t * slots, (t + 1) * slots)
            state[where, lanes] = state[where, lanes] + silu(mixed)

    for m in range(MP):

        @pl.when(place_of[0] == m)
        def _(m=m):
            own[...] = comb[:, :, m * share : (m + 1) * share]

    masks = [jnp.broadcast_to(valid[...] == v, (slots, share)) for v in range(1, CH + 1)]
    for j in range(kept):
        picked = own[j + 1]
        for v in range(2, CH + 1):
            picked = jnp.where(masks[v - 1], own[j + v], picked)
        new_conv[j] = picked.astype(jnp.bfloat16)

    total = state[...]
    ffn_in = norm(total, ffn_gain[...])
    for m in range(MP):
        up = weights[m, share : share + hidden_units, :]
        down = weights[m, share + hidden_units :, :]
        hidden = silu(
            lax.dot_general(
                ffn_in, up, (((1,), (1,)), ((), ())), preferred_element_type=jnp.float32
            )
        )
        total = total + jnp.dot(
            hidden.astype(jnp.bfloat16), down, preferred_element_type=jnp.float32
        )
    if last:
        rounded = total.astype(jnp.bfloat16)
        for m in range(MP):

            @pl.when(place_of[0] == m)
            def _(m=m):
                result[...] = lax.dot_general(
                    rounded[:, m * share : (m + 1) * share],
                    tail[...],
                    (((0,), (1,)), ((), ())),
                    preferred_element_type=jnp.float32,
                ).astype(jnp.bfloat16)

    else:
        state_out[...] = total
        result[...] = lax.dot_general(
            norm(total, next_gain[...]),
            tail[...],
            (((1,), (1,)), ((), ())),
            preferred_element_type=jnp.float32,
        ).astype(jnp.bfloat16)


def block(last, state, valid, gains, taps, cache, heads, weights, tail, share):
    frames, width = state.shape
    slots = frames // CH
    vmem = pl.BlockSpec(memory_space=pltpu.VMEM)
    place_of = lax.axis_index("mp").reshape(1)
    args = [state, valid, *gains, taps, cache, *heads, weights, tail]
    conv_shape = jax.ShapeDtypeStruct((KT - 1, slots, share), jnp.bfloat16)
    if last:
        shapes = [jax.ShapeDtypeStruct((share, frames), jnp.bfloat16), conv_shape]
    else:
        shapes = [
            jax.ShapeDtypeStruct((frames, width), jnp.float32),
            jax.ShapeDtypeStruct((frames, tail.shape[0]), jnp.bfloat16),
            conv_shape,
        ]
    return pl.pallas_call(
        functools.partial(block_kernel, last),
        in_specs=[pl.BlockSpec(memory_space=pltpu.SMEM)] + [vmem] * len(args),
        out_specs=[vmem] * len(shapes),
        out_shape=shapes,
        scratch_shapes=[
            pltpu.VMEM((frames, width), jnp.float32),
            pltpu.VMEM((KT - 1 + CH, slots, width), jnp.float32),
            pltpu.VMEM((KT - 1 + CH, slots, share), jnp.float32),
        ],
        compiler_params=pltpu.CompilerParams(vmem_limit_bytes=VMEM_LIMIT),
        name="block",
    )(place_of, *args)


def local(
    features,
    block_valid_frames,
    feature_running_mean,
    feature_running_variance,
    frames_counted,
    slot_relocation,
    speaker,
    speaker_adapter_row,
    adapter_down_panels,
    adapter_up_panels,
    input_weight,
    attention_norm_gain,
    query_key_value_weight,
    attention_output_weight,
    convolution_norm_gain,
    depthwise_taps,
    feedforward_norm_gain,
    up_weight,
    down_weight,
    key_value_cache,
    convolution_cache,
):
    slots = key_value_cache.shape[0]
    peers = lax.axis_size("streams")
    me = lax.axis_index("streams")
    mp = lax.axis_index("mp")
    first = me * slots
    held = adapter_down_panels.shape[0]
    width = input_weight.shape[1]
    heads = key_value_cache.shape[3]
    rows = slots * CH

    spread, begin_by_steps, pick_in_order, begin_at_once, finish, settle = move_caches(
        key_value_cache, convolution_cache, slot_relocation
    )

    small = jnp.concatenate(
        [
            attention_norm_gain,
            convolution_norm_gain,
            feedforward_norm_gain,
            depthwise_taps.reshape(LAYERS * KT, width),
        ],
        axis=0,
    )
    small = side_by_side(ring(small))
    weights = []
    for l in range(LAYERS):
        mine = [attention_output_weight[l], jnp.transpose(up_weight[l]), down_weight[l]]
        weights.append(lax.all_gather(jnp.concatenate(mine, axis=0), "mp", axis=0))
    qkv_w = []
    for l in range(LAYERS):
        w = jnp.transpose(query_key_value_weight[l], (1, 2, 0))
        w = w.reshape(3, heads, HEAD_DIM, MODEL_WIDTH)
        pairs = jnp.stack(
            [
                jnp.stack([w[0], jnp.zeros_like(w[0])], axis=1),
                jnp.stack([w[1], w[2]], axis=1),
            ]
        )
        qkv_w.append(pairs.reshape(4 * heads * HEAD_DIM, MODEL_WIDTH))

    ids = jnp.arange(speaker_adapter_row.shape[0], dtype=jnp.int32)
    all_rows = jnp.sum(
        jnp.where(speaker[:, None] == ids[None, :], speaker_adapter_row[None, :], 0), axis=1
    )
    asked = all_rows.reshape(peers, slots)
    give = jnp.sum(jnp.where(asked // held == me, asked % held, 0), axis=1)
    my_rows = lax.dynamic_slice_in_dim(all_rows, first, slots, 0)
    flat_down = adapter_down_panels.reshape(held, -1, 128)
    flat_up = adapter_up_panels.reshape(held, -1, 128)
    panels = jnp.concatenate([flat_up, flat_down], axis=1)
    panels = jnp.take(panels, give, axis=0, mode="clip")
    panels, _ = lax.optimization_barrier((panels, spread))
    spread, small = lax.optimization_barrier((spread, small))
    arrived = begin_by_steps(0, spread)
    got = exchange(panels)
    arrived, got, spread, weights[0] = lax.optimization_barrier(
        (arrived, got, spread, weights[0])
    )
    attn_gain, conv_gain, ffn_gain = small[0:2], small[2:4], small[4:6]
    taps = small[6:].reshape(LAYERS, KT, MODEL_WIDTH)
    part = pick_in_order(1, spread)
    near_got, part = lax.optimization_barrier((finish(arrived), part))
    later = begin_at_once(part)
    got = jnp.take(got, my_rows // held, axis=0, mode="clip")
    panel_up = got[:, : flat_up.shape[1]].reshape((slots,) + adapter_up_panels.shape[1:])
    panel_down = got[:, flat_up.shape[1] :].reshape((slots,) + adapter_down_panels.shape[1:])

    frames = features.reshape(slots, CH, FILTER_CHANNELS)
    positions = jnp.arange(CH, dtype=jnp.int32)
    live = (positions[None, :] < block_valid_frames[:, None]).astype(jnp.float32)[:, :, None]
    seen_here = frames_counted[:, None]
    counted = seen_here + block_valid_frames.astype(jnp.float32)[:, None]
    new_mean = (seen_here * feature_running_mean + jnp.sum(live * frames, axis=1)) / counted
    centred = frames - new_mean[:, None, :]
    shifted = feature_running_mean - new_mean
    new_var = (
        seen_here * (feature_running_variance + shifted * shifted)
        + jnp.sum(live * centred * centred, axis=1)
    ) / counted
    normed = (centred / jnp.sqrt(new_var + CMVN_EPS)[:, None, :]).astype(jnp.bfloat16)
    low = jnp.einsum("stm,srm->str", normed, panel_down, preferred_element_type=jnp.float32).astype(
        jnp.bfloat16
    )
    part = dot(normed.reshape(rows, FILTER_CHANNELS), input_weight)
    part = part + jnp.einsum(
        "str,src->stc", low, panel_up, preferred_element_type=jnp.float32
    ).reshape(rows, width)
    part = jnp.transpose(part.reshape(slots, CH, width), (1, 0, 2)).reshape(rows, width)
    state = side_by_side(ring(part))

    row = jnp.arange(rows, dtype=jnp.int32)
    row_slot, row_frame = row // CH, row % CH
    order = (row[None, :] == (row_frame * slots + row_slot)[:, None]).astype(jnp.bfloat16)
    column = jnp.arange(4 * (FR + CH), dtype=jnp.int32)
    fresh = (column % (FR + CH) - FR)[None, :]
    allowed = (row_slot % 4)[:, None] == (column // (FR + CH))[None, :]
    row_valid = jnp.repeat(block_valid_frames, CH)[:, None]
    allowed = allowed & ((fresh < 0) | (fresh <= row_frame[:, None]) & (fresh < row_valid))
    bias = jnp.where(allowed, 0.0, -1e30).astype(jnp.float32)
    valid = block_valid_frames[:, None]

    qkv = lax.dot_general(
        norm(state, attn_gain[0]),
        qkv_w[0],
        (((1,), (1,)), ((), ())),
        preferred_element_type=jnp.float32,
    ).astype(jnp.bfloat16)
    kv_out = None
    conv_out = []
    for layer in range(LAYERS):
        last = layer == LAYERS - 1
        if last:
            later, state, qkv, weights[1] = lax.optimization_barrier(
                (later, state, qkv, weights[1])
            )
            near_got = finish(later)
        got, conv_own = settle(layer, near_got)
        heads_out, kv_out = attention(
            layer, block_valid_frames, order, bias, qkv, got, kv_out, heads
        )
        cache = side_by_side(ring(conv_own))
        following = 0 if last else layer + 1
        gains = [
            conv_gain[layer : layer + 1],
            ffn_gain[layer : layer + 1],
            attn_gain[following : following + 1],
        ]
        done = block(
            last,
            state,
            valid,
            gains,
            taps[layer],
            cache,
            ring(heads_out),
            weights[layer],
            order if last else qkv_w[layer + 1],
            width,
        )
        conv_out.append(done[-1])
        if last:
            enc_out = done[0]
        else:
            state, qkv = done[0], done[1]
    return (
        enc_out,
        jnp.transpose(kv_out, (0, 1, 3, 2, 4)),
        jnp.transpose(jnp.stack(conv_out), (2, 0, 1, 3)),
        new_mean,
        new_var,
    )


def solution(mesh):
    return jax.shard_map(
        local,
        mesh=mesh,
        in_specs=(
            P("streams", None),
            P("streams"),
            P("streams", None),
            P("streams", None),
            P("streams"),
            P(),
            P(),
            P(),
            P("streams", None, None),
            P("streams", None, "mp"),
            P(None, "mp"),
            P(None, "mp"),
            P(None, None, None, "mp"),
            P(None, "mp", None),
            P(None, "mp"),
            P(None, None, "mp"),
            P(None, "mp"),
            P(None, None, "mp"),
            P(None, "mp", None),
            P("streams", None, None, "mp", None),
            P("streams", None, None, "mp"),
        ),
        out_specs=(
            P("mp", "streams"),
            P("streams", None, None, "mp", None),
            P("streams", None, None, "mp"),
            P("streams", None),
            P("streams", None),
        ),
        check_vma=False,
    )
```

```python
import functools

import jax
import jax.numpy as jnp
from jax import lax
from jax.experimental import pallas as pl
from jax.experimental.pallas import tpu as pltpu
from jax.sharding import PartitionSpec as P

MODEL_WIDTH = 768
HEAD_DIM = 64
FILTER_CHANNELS = 80
FR = 64
KT = 31
CH = 16
LAYERS = 2
MP = 4
HALF = 32
VMEM_LIMIT = 48 * 1024 * 1024

NORM_EPS = 1e-06
CMVN_EPS = 1e-05


def from_peer(x, shift):
    return lax.ppermute(x, "mp", [((i + shift) % MP, i) for i in range(MP)])


def ring(x):
    return [x] + [from_peer(x, s) for s in range(1, MP)]


def norm(state, gain):
    total = jnp.sum(state * state, axis=-1, keepdims=True)
    spread = jnp.sqrt(total / MODEL_WIDTH + NORM_EPS)
    return (state / spread * gain).astype(jnp.bfloat16)


def dot(a, b):
    return lax.dot_general(a, b, (((1,), (0,)), ((), ())), preferred_element_type=jnp.float32)


def exchange(x):
    return lax.all_to_all(x, "streams", split_axis=0, concat_axis=0, tiled=True)


def peers_in_order(parts):
    first = lax.axis_index("mp")
    order = (jnp.arange(MP, dtype=jnp.int32) - first) % MP
    return jnp.take(jnp.stack(parts), order, axis=0, mode="clip")


def side_by_side(parts):
    ordered = peers_in_order(parts)
    return jnp.concatenate([ordered[c] for c in range(MP)], axis=-1)


def pick_kernel(index, pieces, *outs):
    count = outs[0].shape[0]
    for s, out in enumerate(outs):

        @pl.loop(0, count)
        def _(c, s=s, out=out):
            out[c] = pieces[index[s * count + c], 0]


def pick(index, pieces, layer, planes, count):
    slots, layers, rows, lanes = pieces.shape
    return pl.pallas_call(
        pick_kernel,
        grid=(1,),
        in_specs=[
            pl.BlockSpec(memory_space=pltpu.SMEM),
            pl.BlockSpec((slots, 1, rows, lanes), lambda i: (0, layer, 0, 0)),
        ],
        out_specs=[pl.BlockSpec((count, rows, lanes), lambda i: (0, 0, 0))] * planes,
        out_shape=[jax.ShapeDtypeStruct((count, rows, lanes), pieces.dtype)] * planes,
        compiler_params=pltpu.CompilerParams(vmem_limit_bytes=VMEM_LIMIT),
        name="pick",
    )(index, pieces)


def place_kernel(index, *refs):
    out = refs[-1]
    count = refs[0].shape[0]
    for s, got in enumerate(refs[:-1]):

        @pl.loop(0, count)
        def _(c, s=s, got=got):
            spot = index[s * count + c]

            @pl.when(spot < out.shape[0])
            def _():
                out[spot] = got[c]


def place(index, arrived, slots):
    _, rows, lanes = arrived[0].shape
    return pl.pallas_call(
        place_kernel,
        in_specs=[pl.BlockSpec(memory_space=pltpu.SMEM)]
        + [pl.BlockSpec(memory_space=pltpu.VMEM)] * len(arrived),
        out_specs=pl.BlockSpec(memory_space=pltpu.VMEM),
        out_shape=jax.ShapeDtypeStruct((slots, rows, lanes), arrived[0].dtype),
        compiler_params=pltpu.CompilerParams(vmem_limit_bytes=VMEM_LIMIT),
        name="place",
    )(index, *arrived)


def move_caches(key_value_cache, convolution_cache, slot_relocation):
    slots = key_value_cache.shape[0]
    peers = lax.axis_size("streams")
    me = lax.axis_index("streams")
    group = 8 if peers % 8 == 0 else 2
    planes = peers // group
    plane_slots = group * slots
    room = plane_slots * 7 // 32 if planes > 2 else plane_slots // 2
    plane = me // group
    near = [[p * group + j for j in range(group)] for p in range(planes)]

    goes = (slot_relocation // plane_slots).reshape(planes, plane_slots)
    at = jnp.arange(plane_slots, dtype=jnp.int32)
    same = (goes[:, None, :] == goes[:, :, None]) & (at[None, None, :] < at[None, :, None])
    rank = jnp.sum(same.astype(jnp.int32), axis=2)
    fits = jnp.max(rank) < room
    step = jnp.arange(planes, dtype=jnp.int32)
    c = jnp.arange(room, dtype=jnp.int32)
    my_goes = lax.dynamic_index_in_dim(goes, plane, 0, keepdims=False)
    my_rank = lax.dynamic_index_in_dim(rank, plane, 0, keepdims=False)
    match = (my_goes[None, None, :] == ((plane + step) % planes)[:, None, None]) & (
        my_rank[None, None, :] == c[None, :, None]
    )
    out_index = jnp.sum(jnp.where(match, at[None, None, :], 0), axis=2).reshape(-1)
    origin = (plane - step) % planes
    there_goes = jnp.take(goes, origin, axis=0, mode="clip")
    there_rank = jnp.take(rank, origin, axis=0, mode="clip")
    there_spot = jnp.take(
        (slot_relocation % plane_slots).reshape(planes, plane_slots), origin, axis=0, mode="clip"
    )
    match = (there_goes[:, None, :] == plane) & (there_rank[:, None, :] == c[None, :, None])
    in_index = plane_slots + jnp.sum(
        jnp.where(match, there_spot[:, None, :] - plane_slots, 0), axis=2
    ).reshape(-1)

    heads = key_value_cache.shape[3]
    kv = jnp.transpose(key_value_cache, (0, 1, 3, 2, 4)).reshape(
        slots, LAYERS, group, heads * FR // group, 2 * HEAD_DIM
    )
    taken = convolution_cache.shape[2]
    low = jnp.pad(convolution_cache[..., :128], ((0, 0), (0, 0), (0, HALF - taken), (0, 0)))
    high = jnp.pad(
        convolution_cache[..., 128:],
        ((0, 0), (0, 0), (0, HALF - taken), (0, 256 - convolution_cache.shape[3])),
    )
    conv = jnp.concatenate([low, high], axis=2).reshape(
        slots, LAYERS, group, 2 * HALF // group, 128
    )
    packed = jnp.concatenate([kv, conv], axis=3)
    rows = packed.shape[3]
    spread = lax.all_to_all(
        jnp.transpose(packed, (2, 0, 1, 3, 4)),
        "streams",
        split_axis=0,
        concat_axis=0,
        axis_index_groups=near,
        tiled=True,
    ).reshape(plane_slots, LAYERS, rows, 128)

    mine = jnp.arange(slots, dtype=jnp.int32)
    peer = jnp.arange(peers, dtype=jnp.int32)

    def dense(layer):
        targets = lax.dynamic_slice_in_dim(slot_relocation, me * slots, slots, 0) // slots
        chosen = jnp.sum(jnp.where(peer[:, None] == targets[None, :], mine[None, :], 0), axis=1)
        anchor = jnp.sum(
            jnp.where(
                slot_relocation[None, :] == (me * slots + mine)[:, None],
                jnp.arange(slot_relocation.shape[0], dtype=jnp.int32)[None, :],
                0,
            ),
            axis=1,
        )
        got = exchange(jnp.take(packed[:, layer], chosen, axis=0, mode="clip"))
        return jnp.transpose(jnp.take(got, anchor // slots, axis=0, mode="clip"), (1, 0, 2, 3))

    kv_rows = kv.shape[3]

    def pick_by_step(layer, pieces):
        return pick(out_index, pieces, layer, planes, room)

    def begin_by_steps(parts):
        arrived = [parts[0]]
        for s in range(1, planes):
            hop = [
                (p * group + j, (p + s) % planes * group + j)
                for p in range(planes)
                for j in range(group)
            ]
            arrived.append(lax.ppermute(parts[s], "streams", hop))
        return arrived

    def pick_in_order(layer, pieces):
        index = jnp.take(out_index.reshape(planes, room), (step - plane) % planes, axis=0, mode="clip")
        return pick(index.reshape(-1), pieces, layer, 1, planes * room)[0]

    def begin_at_once(part):
        far = [[p * group + j for p in range(planes)] for j in range(group)]
        return lax.all_to_all(
            part, "streams", split_axis=0, concat_axis=0, axis_index_groups=far, tiled=True
        )

    def finish(arrived):
        index = in_index
        if not isinstance(arrived, list):
            index = jnp.take(index.reshape(planes, room), (plane - step) % planes, axis=0, mode="clip")
            index, arrived = index.reshape(-1), [arrived]
        here = place(index, arrived, plane_slots).reshape(group, slots, rows, 128)
        return lax.all_to_all(
            here, "streams", split_axis=0, concat_axis=0, axis_index_groups=near, tiled=True
        )

    def settle(layer, got):
        got = lax.cond(fits, lambda x: x, lambda x: dense(layer), got)
        c = jnp.transpose(got[:, :, kv_rows:], (0, 2, 1, 3)).reshape(2, HALF, slots, 128)
        own = jnp.concatenate(
            [c[0, :taken], c[1, :taken, :, : convolution_cache.shape[3] - 128]], axis=-1
        )
        return got, own

    return packed, spread, pick_by_step, begin_by_steps, pick_in_order, begin_at_once, finish, settle


def attention_kernel(valid, order, bias, qkv, got, *rest):
    heads_out, kv_out, both, sorted_rows, packed = rest[-5:]
    group, slots, rows, lanes = got.shape
    heads = both.shape[1]
    kv_rows = heads * FR // group

    sorted_rows[...] = jnp.dot(
        order[...], qkv[...], preferred_element_type=jnp.float32
    ).astype(jnp.bfloat16)

    @pl.loop(0, slots)
    def _(s):
        for p in range(group):
            piece = got[p, s].astype(jnp.float32)
            for r in range(0, kv_rows, 8):
                q = p * kv_rows + r
                both[s, q // FR, q % FR : q % FR + 8, :] = piece[r : r + 8]
        new = sorted_rows[pl.ds(pl.multiple_of(s * CH, CH), CH), heads * lanes :]
        for h in range(heads):
            both[s, h, FR:, :] = new[:, h * lanes : (h + 1) * lanes].astype(jnp.float32)
            kv_out[s, 0, h] = both[s, h, pl.ds(valid[s], FR), :].astype(jnp.bfloat16)

    step = 4
    span = step * CH
    lane = lax.broadcasted_iota(jnp.int32, (span, lanes), 1)
    for g in range(slots // step):
        part = slice(g * span, (g + 1) * span)
        outs = []
        for h in range(heads):
            keys = both[g * step : (g + 1) * step, h].reshape(step * (FR + CH), lanes)
            keys = keys.astype(jnp.bfloat16)
            q = sorted_rows[part, h * lanes : (h + 1) * lanes]
            scores = lax.dot_general(
                q, keys, (((1,), (1,)), ((), ())), preferred_element_type=jnp.float32
            )
            scores = scores * HEAD_DIM ** (-0.5) + bias[part, :]
            peak = jnp.max(scores, axis=-1, keepdims=True)
            weights = jnp.exp(scores - peak)
            probs = (weights / jnp.sum(weights, axis=-1, keepdims=True)).astype(jnp.bfloat16)
            outs.append(jnp.dot(probs, keys, preferred_element_type=jnp.float32))
        first = jnp.where(lane < HEAD_DIM, pltpu.roll(outs[0], HEAD_DIM, 1), outs[1])
        second = pltpu.roll(outs[2], HEAD_DIM, 1)
        packed[part, :] = jnp.concatenate([first, second], axis=1).astype(jnp.bfloat16)
    back = lax.dot_general(
        order[...], packed[...], (((0,), (0,)), ((), ())), preferred_element_type=jnp.float32
    )
    heads_out[...] = back[:, : heads_out.shape[1]].astype(jnp.bfloat16)


def attention(layer, valid, order, bias, qkv, got, kv_so_far, heads):
    group, slots, rows, lanes = got.shape
    frames = qkv.shape[0]
    vmem = pl.BlockSpec(memory_space=pltpu.VMEM)
    more = [] if kv_so_far is None else [kv_so_far]
    return pl.pallas_call(
        attention_kernel,
        grid=(1,),
        in_specs=[pl.BlockSpec(memory_space=pltpu.SMEM)]
        + [vmem] * 4
        + [pl.BlockSpec(memory_space=pl.ANY)] * len(more),
        out_specs=[
            vmem,
            pl.BlockSpec((slots, 1, heads, FR, lanes), lambda i: (0, layer, 0, 0, 0)),
        ],
        out_shape=[
            jax.ShapeDtypeStruct((frames, heads * HEAD_DIM), jnp.bfloat16),
            jax.ShapeDtypeStruct((slots, LAYERS, heads, FR, lanes), jnp.bfloat16),
        ],
        scratch_shapes=[
            pltpu.VMEM((slots, heads, FR + CH, lanes), jnp.float32),
            pltpu.VMEM(qkv.shape, jnp.bfloat16),
            pltpu.VMEM((frames, 2 * lanes), jnp.bfloat16),
        ],
        input_output_aliases={5: 1} if more else {},
        compiler_params=pltpu.CompilerParams(vmem_limit_bytes=VMEM_LIMIT),
        name="attention",
    )(valid, order, bias, qkv, got, *more)


def silu(v):
    return v / (1.0 + jnp.exp(-v))


def block_kernel(last, place_of, state_in, valid, conv_gain, ffn_gain, next_gain, taps, cache, *rest):
    heads, (weights, tail), rest = rest[0:MP], rest[MP : MP + 2], rest[MP + 2 :]
    if last:
        result, new_conv, state, comb, own = rest
    else:
        state_out, result, new_conv, state, comb, own = rest
    frames, width = state_in.shape
    slots = frames // CH
    share = new_conv.shape[2]
    kept = KT - 1

    hidden_units = (weights.shape[1] - share) // 2
    total = state_in[...]
    for s, h in enumerate(heads):
        w = weights[(place_of[0] + s) % MP, :share, :]
        total = total + jnp.dot(h[...], w, preferred_element_type=jnp.float32)
    state[...] = total
    conv_in = norm(total, conv_gain[...])
    comb[kept:] = conv_in.astype(jnp.float32).reshape(CH, slots, width)
    comb[:kept] = cache[...].astype(jnp.float32)

    @pl.loop(0, width // 128)
    def _(c):
        lanes = pl.ds(pl.multiple_of(c * 128, 128), 128)
        for t in range(CH):
            mixed = taps[0:1, lanes] * comb[t, :, lanes]
            for k in range(1, KT):
                mixed = mixed + taps[k : k + 1, lanes] * comb[t + k, :, lanes]
            where = slice(t * slots, (t + 1) * slots)
            state[where, lanes] = state[where, lanes] + silu(mixed)

    for m in range(MP):

        @pl.when(place_of[0] == m)
        def _(m=m):
            own[...] = comb[:, :, m * share : (m + 1) * share]

    masks = [jnp.broadcast_to(valid[...] == v, (slots, share)) for v in range(1, CH + 1)]
    for j in range(kept):
        picked = own[j + 1]
        for v in range(2, CH + 1):
            picked = jnp.where(masks[v - 1], own[j + v], picked)
        new_conv[j] = picked.astype(jnp.bfloat16)

    total = state[...]
    ffn_in = norm(total, ffn_gain[...])
    for m in range(MP):
        up = weights[m, share : share + hidden_units, :]
        down = weights[m, share + hidden_units :, :]
        hidden = silu(
            lax.dot_general(
                ffn_in, up, (((1,), (1,)), ((), ())), preferred_element_type=jnp.float32
            )
        )
        total = total + jnp.dot(
            hidden.astype(jnp.bfloat16), down, preferred_element_type=jnp.float32
        )
    if last:
        rounded = total.astype(jnp.bfloat16)
        for m in range(MP):

            @pl.when(place_of[0] == m)
            def _(m=m):
                result[...] = lax.dot_general(
                    rounded[:, m * share : (m + 1) * share],
                    tail[...],
                    (((0,), (1,)), ((), ())),
                    preferred_element_type=jnp.float32,
                ).astype(jnp.bfloat16)

    else:
        state_out[...] = total
        result[...] = lax.dot_general(
            norm(total, next_gain[...]),
            tail[...],
            (((1,), (1,)), ((), ())),
            preferred_element_type=jnp.float32,
        ).astype(jnp.bfloat16)


def block(last, state, valid, gains, taps, cache, heads, weights, tail, share):
    frames, width = state.shape
    slots = frames // CH
    vmem = pl.BlockSpec(memory_space=pltpu.VMEM)
    place_of = lax.axis_index("mp").reshape(1)
    args = [state, valid, *gains, taps, cache, *heads, weights, tail]
    conv_shape = jax.ShapeDtypeStruct((KT - 1, slots, share), jnp.bfloat16)
    if last:
        shapes = [jax.ShapeDtypeStruct((share, frames), jnp.bfloat16), conv_shape]
    else:
        shapes = [
            jax.ShapeDtypeStruct((frames, width), jnp.float32),
            jax.ShapeDtypeStruct((frames, tail.shape[0]), jnp.bfloat16),
            conv_shape,
        ]
    return pl.pallas_call(
        functools.partial(block_kernel, last),
        in_specs=[pl.BlockSpec(memory_space=pltpu.SMEM)] + [vmem] * len(args),
        out_specs=[vmem] * len(shapes),
        out_shape=shapes,
        scratch_shapes=[
            pltpu.VMEM((frames, width), jnp.float32),
            pltpu.VMEM((KT - 1 + CH, slots, width), jnp.float32),
            pltpu.VMEM((KT - 1 + CH, slots, share), jnp.float32),
        ],
        compiler_params=pltpu.CompilerParams(vmem_limit_bytes=VMEM_LIMIT),
        name="block",
    )(place_of, *args)


def local(
    features,
    block_valid_frames,
    feature_running_mean,
    feature_running_variance,
    frames_counted,
    slot_relocation,
    speaker,
    speaker_adapter_row,
    adapter_down_panels,
    adapter_up_panels,
    input_weight,
    attention_norm_gain,
    query_key_value_weight,
    attention_output_weight,
    convolution_norm_gain,
    depthwise_taps,
    feedforward_norm_gain,
    up_weight,
    down_weight,
    key_value_cache,
    convolution_cache,
):
    slots = key_value_cache.shape[0]
    peers = lax.axis_size("streams")
    me = lax.axis_index("streams")
    mp = lax.axis_index("mp")
    first = me * slots
    held = adapter_down_panels.shape[0]
    width = input_weight.shape[1]
    heads = key_value_cache.shape[3]
    rows = slots * CH

    (
        packed,
        spread,
        pick_by_step,
        begin_by_steps,
        pick_in_order,
        begin_at_once,
        finish,
        settle,
    ) = move_caches(key_value_cache, convolution_cache, slot_relocation)

    small = jnp.concatenate(
        [
            attention_norm_gain,
            convolution_norm_gain,
            feedforward_norm_gain,
            depthwise_taps.reshape(LAYERS * KT, width),
        ],
        axis=0,
    )
    small, _ = lax.optimization_barrier((small, packed))
    small = side_by_side(ring(small))
    weights = []
    for l in range(LAYERS):
        mine = [attention_output_weight[l], jnp.transpose(up_weight[l]), down_weight[l]]
        weights.append(lax.all_gather(jnp.concatenate(mine, axis=0), "mp", axis=0))
    qkv_w = []
    for l in range(LAYERS):
        w = jnp.transpose(query_key_value_weight[l], (1, 2, 0))
        w = w.reshape(3, heads, HEAD_DIM, MODEL_WIDTH)
        pairs = jnp.stack(
            [
                jnp.stack([w[0], jnp.zeros_like(w[0])], axis=1),
                jnp.stack([w[1], w[2]], axis=1),
            ]
        )
        qkv_w.append(pairs.reshape(4 * heads * HEAD_DIM, MODEL_WIDTH))

    ids = jnp.arange(speaker_adapter_row.shape[0], dtype=jnp.int32)
    all_rows = jnp.sum(
        jnp.where(speaker[:, None] == ids[None, :], speaker_adapter_row[None, :], 0), axis=1
    )
    asked = all_rows.reshape(peers, slots)
    give = jnp.sum(jnp.where(asked // held == me, asked % held, 0), axis=1)
    my_rows = lax.dynamic_slice_in_dim(all_rows, first, slots, 0)
    flat_down = adapter_down_panels.reshape(held, -1, 128)
    flat_up = adapter_up_panels.reshape(held, -1, 128)
    panels = jnp.concatenate([flat_up, flat_down], axis=1)
    panels = jnp.take(panels, give, axis=0, mode="clip")
    spread, small = lax.optimization_barrier((spread, small))
    parts, panels = lax.optimization_barrier((pick_by_step(0, spread), panels))
    arrived = begin_by_steps(parts)
    got = exchange(panels)
    arrived, spread, weights[0] = lax.optimization_barrier((arrived, spread, weights[0]))
    attn_gain, conv_gain, ffn_gain = small[0:2], small[2:4], small[4:6]
    taps = small[6:].reshape(LAYERS, KT, MODEL_WIDTH)
    near_got = finish(arrived)
    second = pick_in_order(1, spread)
    got = jnp.take(got, my_rows // held, axis=0, mode="clip")
    panel_up = got[:, : flat_up.shape[1]].reshape((slots,) + adapter_up_panels.shape[1:])
    panel_down = got[:, flat_up.shape[1] :].reshape((slots,) + adapter_down_panels.shape[1:])

    frames = features.reshape(slots, CH, FILTER_CHANNELS)
    positions = jnp.arange(CH, dtype=jnp.int32)
    live = (positions[None, :] < block_valid_frames[:, None]).astype(jnp.float32)[:, :, None]
    seen_here = frames_counted[:, None]
    counted = seen_here + block_valid_frames.astype(jnp.float32)[:, None]
    new_mean = (seen_here * feature_running_mean + jnp.sum(live * frames, axis=1)) / counted
    centred = frames - new_mean[:, None, :]
    shifted = feature_running_mean - new_mean
    new_var = (
        seen_here * (feature_running_variance + shifted * shifted)
        + jnp.sum(live * centred * centred, axis=1)
    ) / counted
    normed = (centred / jnp.sqrt(new_var + CMVN_EPS)[:, None, :]).astype(jnp.bfloat16)
    low = jnp.einsum("stm,srm->str", normed, panel_down, preferred_element_type=jnp.float32).astype(
        jnp.bfloat16
    )
    part = dot(normed.reshape(rows, FILTER_CHANNELS), input_weight)
    part = part + jnp.einsum(
        "str,src->stc", low, panel_up, preferred_element_type=jnp.float32
    ).reshape(rows, width)
    part = jnp.transpose(part.reshape(slots, CH, width), (1, 0, 2)).reshape(rows, width)
    state = lax.all_gather(part, "mp", axis=1, tiled=True)

    row = jnp.arange(rows, dtype=jnp.int32)
    row_slot, row_frame = row // CH, row % CH
    order = (row[None, :] == (row_frame * slots + row_slot)[:, None]).astype(jnp.bfloat16)
    column = jnp.arange(4 * (FR + CH), dtype=jnp.int32)
    fresh = (column % (FR + CH) - FR)[None, :]
    allowed = (row_slot % 4)[:, None] == (column // (FR + CH))[None, :]
    row_valid = jnp.repeat(block_valid_frames, CH)[:, None]
    allowed = allowed & ((fresh < 0) | (fresh <= row_frame[:, None]) & (fresh < row_valid))
    bias = jnp.where(allowed, 0.0, -1e30).astype(jnp.float32)
    valid = block_valid_frames[:, None]

    qkv = lax.dot_general(
        norm(state, attn_gain[0]),
        qkv_w[0],
        (((1,), (1,)), ((), ())),
        preferred_element_type=jnp.float32,
    ).astype(jnp.bfloat16)
    near_got, second, state, qkv = lax.optimization_barrier((near_got, second, state, qkv))
    later = begin_at_once(second)
    kv_out = None
    conv_out = []
    for layer in range(LAYERS):
        last = layer == LAYERS - 1
        if last:
            later, state, qkv, weights[1] = lax.optimization_barrier(
                (later, state, qkv, weights[1])
            )
            near_got = finish(later)
        got, conv_own = settle(layer, near_got)
        heads_out, kv_out = attention(
            layer, block_valid_frames, order, bias, qkv, got, kv_out, heads
        )
        cache = side_by_side(ring(conv_own))
        following = 0 if last else layer + 1
        gains = [
            conv_gain[layer : layer + 1],
            ffn_gain[layer : layer + 1],
            attn_gain[following : following + 1],
        ]
        done = block(
            last,
            state,
            valid,
            gains,
            taps[layer],
            cache,
            ring(heads_out),
            weights[layer],
            order if last else qkv_w[layer + 1],
            width,
        )
        conv_out.append(done[-1])
        if last:
            enc_out = done[0]
        else:
            state, qkv = done[0], done[1]
    return (
        enc_out,
        jnp.transpose(kv_out, (0, 1, 3, 2, 4)),
        jnp.transpose(jnp.stack(conv_out), (2, 0, 1, 3)),
        new_mean,
        new_var,
    )


def solution(mesh):
    return jax.shard_map(
        local,
        mesh=mesh,
        in_specs=(
            P("streams", None),
            P("streams"),
            P("streams", None),
            P("streams", None),
            P("streams"),
            P(),
            P(),
            P(),
            P("streams", None, None),
            P("streams", None, "mp"),
            P(None, "mp"),
            P(None, "mp"),
            P(None, None, None, "mp"),
            P(None, "mp", None),
            P(None, "mp"),
            P(None, None, "mp"),
            P(None, "mp"),
            P(None, None, "mp"),
            P(None, "mp", None),
            P("streams", None, None, "mp", None),
            P("streams", None, None, "mp"),
        ),
        out_specs=(
            P("mp", "streams"),
            P("streams", None, None, "mp", None),
            P("streams", None, None, "mp"),
            P("streams", None),
            P("streams", None),
        ),
        check_vma=False,
    )
```

```python
import functools

import jax
import jax.numpy as jnp
from jax import lax
from jax.experimental import pallas as pl
from jax.experimental.pallas import tpu as pltpu
from jax.sharding import PartitionSpec as P

MODEL_WIDTH = 768
HEAD_DIM = 64
FILTER_CHANNELS = 80
FR = 64
KT = 31
CH = 16
LAYERS = 2
MP = 4
HALF = 32
VMEM_LIMIT = 48 * 1024 * 1024

NORM_EPS = 1e-06
CMVN_EPS = 1e-05


def from_peer(x, shift):
    return lax.ppermute(x, "mp", [((i + shift) % MP, i) for i in range(MP)])


def ring(x):
    return [x] + [from_peer(x, s) for s in range(1, MP)]


def norm(state, gain):
    total = jnp.sum(state * state, axis=-1, keepdims=True)
    spread = jnp.sqrt(total / MODEL_WIDTH + NORM_EPS)
    return (state / spread * gain).astype(jnp.bfloat16)


def dot(a, b):
    return lax.dot_general(a, b, (((1,), (0,)), ((), ())), preferred_element_type=jnp.float32)


def exchange(x):
    return lax.all_to_all(x, "streams", split_axis=0, concat_axis=0, tiled=True)


def peers_in_order(parts):
    first = lax.axis_index("mp")
    order = (jnp.arange(MP, dtype=jnp.int32) - first) % MP
    return jnp.take(jnp.stack(parts), order, axis=0, mode="clip")


def side_by_side(parts):
    ordered = peers_in_order(parts)
    return jnp.concatenate([ordered[c] for c in range(MP)], axis=-1)


def pick_kernel(index, pieces, *outs):
    count = outs[0].shape[0]
    for s, out in enumerate(outs):

        @pl.loop(0, count)
        def _(c, s=s, out=out):
            out[c] = pieces[index[s * count + c], 0]


def pick(index, pieces, layer, planes, count):
    slots, layers, rows, lanes = pieces.shape
    return pl.pallas_call(
        pick_kernel,
        grid=(1,),
        in_specs=[
            pl.BlockSpec(memory_space=pltpu.SMEM),
            pl.BlockSpec((slots, 1, rows, lanes), lambda i: (0, layer, 0, 0)),
        ],
        out_specs=[pl.BlockSpec((count, rows, lanes), lambda i: (0, 0, 0))] * planes,
        out_shape=[jax.ShapeDtypeStruct((count, rows, lanes), pieces.dtype)] * planes,
        compiler_params=pltpu.CompilerParams(vmem_limit_bytes=VMEM_LIMIT),
        name="pick",
    )(index, pieces)


def place_kernel(index, *refs):
    out = refs[-1]
    count = refs[0].shape[0]
    for s, got in enumerate(refs[:-1]):

        @pl.loop(0, count)
        def _(c, s=s, got=got):
            spot = index[s * count + c]

            @pl.when(spot < out.shape[0])
            def _():
                out[spot] = got[c]


def place(index, arrived, slots):
    _, rows, lanes = arrived[0].shape
    return pl.pallas_call(
        place_kernel,
        in_specs=[pl.BlockSpec(memory_space=pltpu.SMEM)]
        + [pl.BlockSpec(memory_space=pltpu.VMEM)] * len(arrived),
        out_specs=pl.BlockSpec(memory_space=pltpu.VMEM),
        out_shape=jax.ShapeDtypeStruct((slots, rows, lanes), arrived[0].dtype),
        compiler_params=pltpu.CompilerParams(vmem_limit_bytes=VMEM_LIMIT),
        name="place",
    )(index, *arrived)


def move_caches(key_value_cache, convolution_cache, slot_relocation, after):
    slots = key_value_cache.shape[0]
    peers = lax.axis_size("streams")
    me = lax.axis_index("streams")
    group = 8 if peers % 8 == 0 else 2
    planes = peers // group
    plane_slots = group * slots
    room = plane_slots * 7 // 32 if planes > 2 else plane_slots // 2
    plane = me // group
    near = [[p * group + j for j in range(group)] for p in range(planes)]

    goes = (slot_relocation // plane_slots).reshape(planes, plane_slots)
    at = jnp.arange(plane_slots, dtype=jnp.int32)
    same = (goes[:, None, :] == goes[:, :, None]) & (at[None, None, :] < at[None, :, None])
    rank = jnp.sum(same.astype(jnp.int32), axis=2)
    fits = jnp.max(rank) < room
    step = jnp.arange(planes, dtype=jnp.int32)
    c = jnp.arange(room, dtype=jnp.int32)
    my_goes = lax.dynamic_index_in_dim(goes, plane, 0, keepdims=False)
    my_rank = lax.dynamic_index_in_dim(rank, plane, 0, keepdims=False)
    match = (my_goes[None, None, :] == ((plane + step) % planes)[:, None, None]) & (
        my_rank[None, None, :] == c[None, :, None]
    )
    out_index = jnp.sum(jnp.where(match, at[None, None, :], 0), axis=2).reshape(-1)
    origin = (plane - step) % planes
    there_goes = jnp.take(goes, origin, axis=0, mode="clip")
    there_rank = jnp.take(rank, origin, axis=0, mode="clip")
    there_spot = jnp.take(
        (slot_relocation % plane_slots).reshape(planes, plane_slots), origin, axis=0, mode="clip"
    )
    match = (there_goes[:, None, :] == plane) & (there_rank[:, None, :] == c[None, :, None])
    in_index = plane_slots + jnp.sum(
        jnp.where(match, there_spot[:, None, :] - plane_slots, 0), axis=2
    ).reshape(-1)

    heads = key_value_cache.shape[3]
    kv = jnp.transpose(key_value_cache, (0, 1, 3, 2, 4)).reshape(
        slots, LAYERS, group, heads * FR // group, 2 * HEAD_DIM
    )
    taken = convolution_cache.shape[2]
    low = jnp.pad(convolution_cache[..., :128], ((0, 0), (0, 0), (0, HALF - taken), (0, 0)))
    high = jnp.pad(
        convolution_cache[..., 128:],
        ((0, 0), (0, 0), (0, HALF - taken), (0, 256 - convolution_cache.shape[3])),
    )
    conv = jnp.concatenate([low, high], axis=2).reshape(
        slots, LAYERS, group, 2 * HALF // group, 128
    )
    packed = jnp.concatenate([kv, conv], axis=3)
    rows = packed.shape[3]
    cut, _ = lax.optimization_barrier((jnp.transpose(packed, (2, 0, 1, 3, 4)), after))
    spread = lax.all_to_all(
        cut,
        "streams",
        split_axis=0,
        concat_axis=0,
        axis_index_groups=near,
        tiled=True,
    ).reshape(plane_slots, LAYERS, rows, 128)

    mine = jnp.arange(slots, dtype=jnp.int32)
    peer = jnp.arange(peers, dtype=jnp.int32)

    def dense(layer):
        targets = lax.dynamic_slice_in_dim(slot_relocation, me * slots, slots, 0) // slots
        chosen = jnp.sum(jnp.where(peer[:, None] == targets[None, :], mine[None, :], 0), axis=1)
        anchor = jnp.sum(
            jnp.where(
                slot_relocation[None, :] == (me * slots + mine)[:, None],
                jnp.arange(slot_relocation.shape[0], dtype=jnp.int32)[None, :],
                0,
            ),
            axis=1,
        )
        got = exchange(jnp.take(packed[:, layer], chosen, axis=0, mode="clip"))
        return jnp.transpose(jnp.take(got, anchor // slots, axis=0, mode="clip"), (1, 0, 2, 3))

    kv_rows = kv.shape[3]

    def pick_in_order(layer, pieces):
        index = jnp.take(out_index.reshape(planes, room), (step - plane) % planes, axis=0, mode="clip")
        return pick(index.reshape(-1), pieces, layer, 1, planes * room)[0]

    def begin_at_once(part):
        far = [[p * group + j for p in range(planes)] for j in range(group)]
        return lax.all_to_all(
            part, "streams", split_axis=0, concat_axis=0, axis_index_groups=far, tiled=True
        )

    def finish(arrived):
        index = jnp.take(in_index.reshape(planes, room), (plane - step) % planes, axis=0, mode="clip")
        here = place(index.reshape(-1), [arrived], plane_slots).reshape(group, slots, rows, 128)
        return lax.all_to_all(
            here, "streams", split_axis=0, concat_axis=0, axis_index_groups=near, tiled=True
        )

    def settle(layer, got):
        got = lax.cond(fits, lambda x: x, lambda x: dense(layer), got)
        c = jnp.transpose(got[:, :, kv_rows:], (0, 2, 1, 3)).reshape(2, HALF, slots, 128)
        own = jnp.concatenate(
            [c[0, :taken], c[1, :taken, :, : convolution_cache.shape[3] - 128]], axis=-1
        )
        return got, own

    return packed, spread, pick_in_order, begin_at_once, finish, settle


def attention_kernel(valid, order, bias, qkv, got, *rest):
    heads_out, kv_out, both, sorted_rows, packed = rest[-5:]
    group, slots, rows, lanes = got.shape
    heads = both.shape[1]
    kv_rows = heads * FR // group

    sorted_rows[...] = jnp.dot(
        order[...], qkv[...], preferred_element_type=jnp.float32
    ).astype(jnp.bfloat16)

    @pl.loop(0, slots)
    def _(s):
        for p in range(group):
            piece = got[p, s].astype(jnp.float32)
            for r in range(0, kv_rows, 8):
                q = p * kv_rows + r
                both[s, q // FR, q % FR : q % FR + 8, :] = piece[r : r + 8]
        new = sorted_rows[pl.ds(pl.multiple_of(s * CH, CH), CH), heads * lanes :]
        for h in range(heads):
            both[s, h, FR:, :] = new[:, h * lanes : (h + 1) * lanes].astype(jnp.float32)
            kv_out[s, 0, h] = both[s, h, pl.ds(valid[s], FR), :].astype(jnp.bfloat16)

    step = 4
    span = step * CH
    lane = lax.broadcasted_iota(jnp.int32, (span, lanes), 1)
    for g in range(slots // step):
        part = slice(g * span, (g + 1) * span)
        outs = []
        for h in range(heads):
            keys = both[g * step : (g + 1) * step, h].reshape(step * (FR + CH), lanes)
            keys = keys.astype(jnp.bfloat16)
            q = sorted_rows[part, h * lanes : (h + 1) * lanes]
            scores = lax.dot_general(
                q, keys, (((1,), (1,)), ((), ())), preferred_element_type=jnp.float32
            )
            scores = scores * HEAD_DIM ** (-0.5) + bias[part, :]
            peak = jnp.max(scores, axis=-1, keepdims=True)
            weights = jnp.exp(scores - peak)
            probs = (weights / jnp.sum(weights, axis=-1, keepdims=True)).astype(jnp.bfloat16)
            outs.append(jnp.dot(probs, keys, preferred_element_type=jnp.float32))
        first = jnp.where(lane < HEAD_DIM, pltpu.roll(outs[0], HEAD_DIM, 1), outs[1])
        second = pltpu.roll(outs[2], HEAD_DIM, 1)
        packed[part, :] = jnp.concatenate([first, second], axis=1).astype(jnp.bfloat16)
    back = lax.dot_general(
        order[...], packed[...], (((0,), (0,)), ((), ())), preferred_element_type=jnp.float32
    )
    heads_out[...] = back[:, : heads_out.shape[1]].astype(jnp.bfloat16)


def attention(layer, valid, order, bias, qkv, got, kv_so_far, heads):
    group, slots, rows, lanes = got.shape
    frames = qkv.shape[0]
    vmem = pl.BlockSpec(memory_space=pltpu.VMEM)
    more = [] if kv_so_far is None else [kv_so_far]
    return pl.pallas_call(
        attention_kernel,
        grid=(1,),
        in_specs=[pl.BlockSpec(memory_space=pltpu.SMEM)]
        + [vmem] * 4
        + [pl.BlockSpec(memory_space=pl.ANY)] * len(more),
        out_specs=[
            vmem,
            pl.BlockSpec((slots, 1, heads, FR, lanes), lambda i: (0, layer, 0, 0, 0)),
        ],
        out_shape=[
            jax.ShapeDtypeStruct((frames, heads * HEAD_DIM), jnp.bfloat16),
            jax.ShapeDtypeStruct((slots, LAYERS, heads, FR, lanes), jnp.bfloat16),
        ],
        scratch_shapes=[
            pltpu.VMEM((slots, heads, FR + CH, lanes), jnp.float32),
            pltpu.VMEM(qkv.shape, jnp.bfloat16),
            pltpu.VMEM((frames, 2 * lanes), jnp.bfloat16),
        ],
        input_output_aliases={5: 1} if more else {},
        compiler_params=pltpu.CompilerParams(vmem_limit_bytes=VMEM_LIMIT),
        name="attention",
    )(valid, order, bias, qkv, got, *more)


def silu(v):
    return v / (1.0 + jnp.exp(-v))


def block_kernel(last, place_of, state_in, valid, conv_gain, ffn_gain, next_gain, taps, cache, *rest):
    heads, (weights, tail), rest = rest[0:MP], rest[MP : MP + 2], rest[MP + 2 :]
    if last:
        result, new_conv, state, comb, own = rest
    else:
        state_out, result, new_conv, state, comb, own = rest
    frames, width = state_in.shape
    slots = frames // CH
    share = new_conv.shape[2]
    kept = KT - 1

    hidden_units = (weights.shape[1] - share) // 2
    total = state_in[...]
    for s, h in enumerate(heads):
        w = weights[(place_of[0] + s) % MP, :share, :]
        total = total + jnp.dot(h[...], w, preferred_element_type=jnp.float32)
    state[...] = total
    conv_in = norm(total, conv_gain[...])
    comb[kept:] = conv_in.astype(jnp.float32).reshape(CH, slots, width)
    comb[:kept] = cache[...].astype(jnp.float32)

    @pl.loop(0, width // 128)
    def _(c):
        lanes = pl.ds(pl.multiple_of(c * 128, 128), 128)
        for t in range(CH):
            mixed = taps[0:1, lanes] * comb[t, :, lanes]
            for k in range(1, KT):
                mixed = mixed + taps[k : k + 1, lanes] * comb[t + k, :, lanes]
            where = slice(t * slots, (t + 1) * slots)
            state[where, lanes] = state[where, lanes] + silu(mixed)

    for m in range(MP):

        @pl.when(place_of[0] == m)
        def _(m=m):
            own[...] = comb[:, :, m * share : (m + 1) * share]

    masks = [jnp.broadcast_to(valid[...] == v, (slots, share)) for v in range(1, CH + 1)]
    for j in range(kept):
        picked = own[j + 1]
        for v in range(2, CH + 1):
            picked = jnp.where(masks[v - 1], own[j + v], picked)
        new_conv[j] = picked.astype(jnp.bfloat16)

    total = state[...]
    ffn_in = norm(total, ffn_gain[...])
    for m in range(MP):
        up = weights[m, share : share + hidden_units, :]
        down = weights[m, share + hidden_units :, :]
        hidden = silu(
            lax.dot_general(
                ffn_in, up, (((1,), (1,)), ((), ())), preferred_element_type=jnp.float32
            )
        )
        total = total + jnp.dot(
            hidden.astype(jnp.bfloat16), down, preferred_element_type=jnp.float32
        )
    if last:
        rounded = total.astype(jnp.bfloat16)
        for m in range(MP):

            @pl.when(place_of[0] == m)
            def _(m=m):
                result[...] = lax.dot_general(
                    rounded[:, m * share : (m + 1) * share],
                    tail[...],
                    (((0,), (1,)), ((), ())),
                    preferred_element_type=jnp.float32,
                ).astype(jnp.bfloat16)

    else:
        state_out[...] = total
        result[...] = lax.dot_general(
            norm(total, next_gain[...]),
            tail[...],
            (((1,), (1,)), ((), ())),
            preferred_element_type=jnp.float32,
        ).astype(jnp.bfloat16)


def block(last, state, valid, gains, taps, cache, heads, weights, tail, share):
    frames, width = state.shape
    slots = frames // CH
    vmem = pl.BlockSpec(memory_space=pltpu.VMEM)
    place_of = lax.axis_index("mp").reshape(1)
    args = [state, valid, *gains, taps, cache, *heads, weights, tail]
    conv_shape = jax.ShapeDtypeStruct((KT - 1, slots, share), jnp.bfloat16)
    if last:
        shapes = [jax.ShapeDtypeStruct((share, frames), jnp.bfloat16), conv_shape]
    else:
        shapes = [
            jax.ShapeDtypeStruct((frames, width), jnp.float32),
            jax.ShapeDtypeStruct((frames, tail.shape[0]), jnp.bfloat16),
            conv_shape,
        ]
    return pl.pallas_call(
        functools.partial(block_kernel, last),
        in_specs=[pl.BlockSpec(memory_space=pltpu.SMEM)] + [vmem] * len(args),
        out_specs=[vmem] * len(shapes),
        out_shape=shapes,
        scratch_shapes=[
            pltpu.VMEM((frames, width), jnp.float32),
            pltpu.VMEM((KT - 1 + CH, slots, width), jnp.float32),
            pltpu.VMEM((KT - 1 + CH, slots, share), jnp.float32),
        ],
        compiler_params=pltpu.CompilerParams(vmem_limit_bytes=VMEM_LIMIT),
        name="block",
    )(place_of, *args)


def local(
    features,
    block_valid_frames,
    feature_running_mean,
    feature_running_variance,
    frames_counted,
    slot_relocation,
    speaker,
    speaker_adapter_row,
    adapter_down_panels,
    adapter_up_panels,
    input_weight,
    attention_norm_gain,
    query_key_value_weight,
    attention_output_weight,
    convolution_norm_gain,
    depthwise_taps,
    feedforward_norm_gain,
    up_weight,
    down_weight,
    key_value_cache,
    convolution_cache,
):
    slots = key_value_cache.shape[0]
    peers = lax.axis_size("streams")
    me = lax.axis_index("streams")
    mp = lax.axis_index("mp")
    first = me * slots
    held = adapter_down_panels.shape[0]
    width = input_weight.shape[1]
    heads = key_value_cache.shape[3]
    rows = slots * CH

    ids = jnp.arange(speaker_adapter_row.shape[0], dtype=jnp.int32)
    all_rows = jnp.sum(
        jnp.where(speaker[:, None] == ids[None, :], speaker_adapter_row[None, :], 0), axis=1
    )
    asked = all_rows.reshape(peers, slots)
    give = jnp.sum(jnp.where(asked // held == me, asked % held, 0), axis=1)
    my_rows = lax.dynamic_slice_in_dim(all_rows, first, slots, 0)
    flat_down = adapter_down_panels.reshape(held, -1, 128)
    flat_up = adapter_up_panels.reshape(held, -1, 128)
    panels = jnp.concatenate([flat_up, flat_down], axis=1)
    panels = jnp.take(panels, give, axis=0, mode="clip")
    got = exchange(panels)

    packed, spread, pick_in_order, begin_at_once, finish, settle = move_caches(
        key_value_cache, convolution_cache, slot_relocation, got
    )

    small = jnp.concatenate(
        [
            attention_norm_gain,
            convolution_norm_gain,
            feedforward_norm_gain,
            depthwise_taps.reshape(LAYERS * KT, width),
        ],
        axis=0,
    )
    small, _ = lax.optimization_barrier((small, packed))
    small = side_by_side(ring(small))
    weights = []
    for l in range(LAYERS):
        mine = [attention_output_weight[l], jnp.transpose(up_weight[l]), down_weight[l]]
        weights.append(lax.all_gather(jnp.concatenate(mine, axis=0), "mp", axis=0))
    qkv_w = []
    for l in range(LAYERS):
        w = jnp.transpose(query_key_value_weight[l], (1, 2, 0))
        w = w.reshape(3, heads, HEAD_DIM, MODEL_WIDTH)
        pairs = jnp.stack(
            [
                jnp.stack([w[0], jnp.zeros_like(w[0])], axis=1),
                jnp.stack([w[1], w[2]], axis=1),
            ]
        )
        qkv_w.append(pairs.reshape(4 * heads * HEAD_DIM, MODEL_WIDTH))

    arrived = begin_at_once(pick_in_order(0, spread))
    arrived, spread, weights[0] = lax.optimization_barrier((arrived, spread, weights[0]))
    attn_gain, conv_gain, ffn_gain = small[0:2], small[2:4], small[4:6]
    taps = small[6:].reshape(LAYERS, KT, MODEL_WIDTH)
    near_got = finish(arrived)
    second = pick_in_order(1, spread)
    got = jnp.take(got, my_rows // held, axis=0, mode="clip")
    panel_up = got[:, : flat_up.shape[1]].reshape((slots,) + adapter_up_panels.shape[1:])
    panel_down = got[:, flat_up.shape[1] :].reshape((slots,) + adapter_down_panels.shape[1:])

    frames = features.reshape(slots, CH, FILTER_CHANNELS)
    positions = jnp.arange(CH, dtype=jnp.int32)
    live = (positions[None, :] < block_valid_frames[:, None]).astype(jnp.float32)[:, :, None]
    seen_here = frames_counted[:, None]
    counted = seen_here + block_valid_frames.astype(jnp.float32)[:, None]
    new_mean = (seen_here * feature_running_mean + jnp.sum(live * frames, axis=1)) / counted
    centred = frames - new_mean[:, None, :]
    shifted = feature_running_mean - new_mean
    new_var = (
        seen_here * (feature_running_variance + shifted * shifted)
        + jnp.sum(live * centred * centred, axis=1)
    ) / counted
    normed = (centred / jnp.sqrt(new_var + CMVN_EPS)[:, None, :]).astype(jnp.bfloat16)
    low = jnp.einsum("stm,srm->str", normed, panel_down, preferred_element_type=jnp.float32).astype(
        jnp.bfloat16
    )
    part = dot(normed.reshape(rows, FILTER_CHANNELS), input_weight)
    part = part + jnp.einsum(
        "str,src->stc", low, panel_up, preferred_element_type=jnp.float32
    ).reshape(rows, width)
    part = jnp.transpose(part.reshape(slots, CH, width), (1, 0, 2)).reshape(rows, width)
    state = lax.all_gather(part, "mp", axis=1, tiled=True)

    row = jnp.arange(rows, dtype=jnp.int32)
    row_slot, row_frame = row // CH, row % CH
    order = (row[None, :] == (row_frame * slots + row_slot)[:, None]).astype(jnp.bfloat16)
    column = jnp.arange(4 * (FR + CH), dtype=jnp.int32)
    fresh = (column % (FR + CH) - FR)[None, :]
    allowed = (row_slot % 4)[:, None] == (column // (FR + CH))[None, :]
    row_valid = jnp.repeat(block_valid_frames, CH)[:, None]
    allowed = allowed & ((fresh < 0) | (fresh <= row_frame[:, None]) & (fresh < row_valid))
    bias = jnp.where(allowed, 0.0, -1e30).astype(jnp.float32)
    valid = block_valid_frames[:, None]

    qkv = lax.dot_general(
        norm(state, attn_gain[0]),
        qkv_w[0],
        (((1,), (1,)), ((), ())),
        preferred_element_type=jnp.float32,
    ).astype(jnp.bfloat16)
    near_got, second, state, qkv = lax.optimization_barrier((near_got, second, state, qkv))
    later = begin_at_once(second)
    kv_out = None
    conv_out = []
    for layer in range(LAYERS):
        last = layer == LAYERS - 1
        if last:
            later, state, qkv, weights[1] = lax.optimization_barrier(
                (later, state, qkv, weights[1])
            )
            near_got = finish(later)
        got, conv_own = settle(layer, near_got)
        heads_out, kv_out = attention(
            layer, block_valid_frames, order, bias, qkv, got, kv_out, heads
        )
        cache = side_by_side(ring(conv_own))
        following = 0 if last else layer + 1
        gains = [
            conv_gain[layer : layer + 1],
            ffn_gain[layer : layer + 1],
            attn_gain[following : following + 1],
        ]
        done = block(
            last,
            state,
            valid,
            gains,
            taps[layer],
            cache,
            ring(heads_out),
            weights[layer],
            order if last else qkv_w[layer + 1],
            width,
        )
        conv_out.append(done[-1])
        if last:
            enc_out = done[0]
        else:
            state, qkv = done[0], done[1]
    return (
        enc_out,
        jnp.transpose(kv_out, (0, 1, 3, 2, 4)),
        jnp.transpose(jnp.stack(conv_out), (2, 0, 1, 3)),
        new_mean,
        new_var,
    )


def solution(mesh):
    return jax.shard_map(
        local,
        mesh=mesh,
        in_specs=(
            P("streams", None),
            P("streams"),
            P("streams", None),
            P("streams", None),
            P("streams"),
            P(),
            P(),
            P(),
            P("streams", None, None),
            P("streams", None, "mp"),
            P(None, "mp"),
            P(None, "mp"),
            P(None, None, None, "mp"),
            P(None, "mp", None),
            P(None, "mp"),
            P(None, None, "mp"),
            P(None, "mp"),
            P(None, None, "mp"),
            P(None, "mp", None),
            P("streams", None, None, "mp", None),
            P("streams", None, None, "mp"),
        ),
        out_specs=(
            P("mp", "streams"),
            P("streams", None, None, "mp", None),
            P("streams", None, None, "mp"),
            P("streams", None),
            P("streams", None),
        ),
        check_vma=False,
    )
```

```python
import functools

import jax
import jax.numpy as jnp
from jax import lax
from jax.experimental import pallas as pl
from jax.experimental.pallas import tpu as pltpu
from jax.sharding import PartitionSpec as P

MODEL_WIDTH = 768
HEAD_DIM = 64
FILTER_CHANNELS = 80
FR = 64
KT = 31
CH = 16
LAYERS = 2
MP = 4
HALF = 32
VMEM_LIMIT = 48 * 1024 * 1024

NORM_EPS = 1e-06
CMVN_EPS = 1e-05


def from_peer(x, shift):
    return lax.ppermute(x, "mp", [((i + shift) % MP, i) for i in range(MP)])


def ring(x):
    return [x] + [from_peer(x, s) for s in range(1, MP)]


def norm(state, gain):
    total = jnp.sum(state * state, axis=-1, keepdims=True)
    spread = jnp.sqrt(total / MODEL_WIDTH + NORM_EPS)
    return (state / spread * gain).astype(jnp.bfloat16)


def dot(a, b):
    return lax.dot_general(a, b, (((1,), (0,)), ((), ())), preferred_element_type=jnp.float32)


def exchange(x):
    return lax.all_to_all(x, "streams", split_axis=0, concat_axis=0, tiled=True)


def peers_in_order(parts):
    first = lax.axis_index("mp")
    order = (jnp.arange(MP, dtype=jnp.int32) - first) % MP
    return jnp.take(jnp.stack(parts), order, axis=0, mode="clip")


def side_by_side(parts):
    ordered = peers_in_order(parts)
    return jnp.concatenate([ordered[c] for c in range(MP)], axis=-1)


def pick_kernel(index, pieces, *outs):
    count = outs[0].shape[0]
    for s, out in enumerate(outs):

        @pl.loop(0, count)
        def _(c, s=s, out=out):
            out[c] = pieces[index[s * count + c], 0]


def pick(index, pieces, layer, planes, count):
    slots, layers, rows, lanes = pieces.shape
    return pl.pallas_call(
        pick_kernel,
        grid=(1,),
        in_specs=[
            pl.BlockSpec(memory_space=pltpu.SMEM),
            pl.BlockSpec((slots, 1, rows, lanes), lambda i: (0, layer, 0, 0)),
        ],
        out_specs=[pl.BlockSpec((count, rows, lanes), lambda i: (0, 0, 0))] * planes,
        out_shape=[jax.ShapeDtypeStruct((count, rows, lanes), pieces.dtype)] * planes,
        compiler_params=pltpu.CompilerParams(vmem_limit_bytes=VMEM_LIMIT),
        name="pick",
    )(index, pieces)


def place_kernel(index, *refs):
    out = refs[-1]
    count = refs[0].shape[0]
    for s, got in enumerate(refs[:-1]):

        @pl.loop(0, count)
        def _(c, s=s, got=got):
            spot = index[s * count + c]

            @pl.when(spot < out.shape[0])
            def _():
                out[spot] = got[c]


def place(index, arrived, slots):
    _, rows, lanes = arrived[0].shape
    return pl.pallas_call(
        place_kernel,
        in_specs=[pl.BlockSpec(memory_space=pltpu.SMEM)]
        + [pl.BlockSpec(memory_space=pltpu.VMEM)] * len(arrived),
        out_specs=pl.BlockSpec(memory_space=pltpu.VMEM),
        out_shape=jax.ShapeDtypeStruct((slots, rows, lanes), arrived[0].dtype),
        compiler_params=pltpu.CompilerParams(vmem_limit_bytes=VMEM_LIMIT),
        name="place",
    )(index, *arrived)


def move_caches(key_value_cache, convolution_cache, slot_relocation):
    slots = key_value_cache.shape[0]
    peers = lax.axis_size("streams")
    me = lax.axis_index("streams")
    group = 8 if peers % 8 == 0 else 2
    planes = peers // group
    plane_slots = group * slots
    room = plane_slots * 7 // 32 if planes > 2 else plane_slots // 2
    plane = me // group
    near = [[p * group + j for j in range(group)] for p in range(planes)]

    goes = (slot_relocation // plane_slots).reshape(planes, plane_slots)
    at = jnp.arange(plane_slots, dtype=jnp.int32)
    same = (goes[:, None, :] == goes[:, :, None]) & (at[None, None, :] < at[None, :, None])
    rank = jnp.sum(same.astype(jnp.int32), axis=2)
    fits = jnp.max(rank) < room
    step = jnp.arange(planes, dtype=jnp.int32)
    c = jnp.arange(room, dtype=jnp.int32)
    my_goes = lax.dynamic_index_in_dim(goes, plane, 0, keepdims=False)
    my_rank = lax.dynamic_index_in_dim(rank, plane, 0, keepdims=False)
    match = (my_goes[None, None, :] == ((plane + step) % planes)[:, None, None]) & (
        my_rank[None, None, :] == c[None, :, None]
    )
    out_index = jnp.sum(jnp.where(match, at[None, None, :], 0), axis=2).reshape(-1)
    origin = (plane - step) % planes
    there_goes = jnp.take(goes, origin, axis=0, mode="clip")
    there_rank = jnp.take(rank, origin, axis=0, mode="clip")
    there_spot = jnp.take(
        (slot_relocation % plane_slots).reshape(planes, plane_slots), origin, axis=0, mode="clip"
    )
    match = (there_goes[:, None, :] == plane) & (there_rank[:, None, :] == c[None, :, None])
    in_index = plane_slots + jnp.sum(
        jnp.where(match, there_spot[:, None, :] - plane_slots, 0), axis=2
    ).reshape(-1)

    heads = key_value_cache.shape[3]
    kv = jnp.transpose(key_value_cache, (0, 1, 3, 2, 4)).reshape(
        slots, LAYERS, group, heads * FR // group, 2 * HEAD_DIM
    )
    taken = convolution_cache.shape[2]
    low = jnp.pad(convolution_cache[..., :128], ((0, 0), (0, 0), (0, HALF - taken), (0, 0)))
    high = jnp.pad(
        convolution_cache[..., 128:],
        ((0, 0), (0, 0), (0, HALF - taken), (0, 256 - convolution_cache.shape[3])),
    )
    conv = jnp.concatenate([low, high], axis=2).reshape(
        slots, LAYERS, group, 2 * HALF // group, 128
    )
    packed = jnp.concatenate([kv, conv], axis=3)
    rows = packed.shape[3]
    spread = lax.all_to_all(
        jnp.transpose(packed, (2, 0, 1, 3, 4)),
        "streams",
        split_axis=0,
        concat_axis=0,
        axis_index_groups=near,
        tiled=True,
    ).reshape(plane_slots, LAYERS, rows, 128)

    mine = jnp.arange(slots, dtype=jnp.int32)
    peer = jnp.arange(peers, dtype=jnp.int32)

    def dense(layer):
        targets = lax.dynamic_slice_in_dim(slot_relocation, me * slots, slots, 0) // slots
        chosen = jnp.sum(jnp.where(peer[:, None] == targets[None, :], mine[None, :], 0), axis=1)
        anchor = jnp.sum(
            jnp.where(
                slot_relocation[None, :] == (me * slots + mine)[:, None],
                jnp.arange(slot_relocation.shape[0], dtype=jnp.int32)[None, :],
                0,
            ),
            axis=1,
        )
        got = exchange(jnp.take(packed[:, layer], chosen, axis=0, mode="clip"))
        return jnp.transpose(jnp.take(got, anchor // slots, axis=0, mode="clip"), (1, 0, 2, 3))

    kv_rows = kv.shape[3]

    def pick_by_step(layer, pieces):
        return pick(out_index, pieces, layer, planes, room)

    def begin_by_steps(parts):
        arrived = [parts[0]]
        for s in range(1, planes):
            hop = [
                (p * group + j, (p + s) % planes * group + j)
                for p in range(planes)
                for j in range(group)
            ]
            arrived.append(lax.ppermute(parts[s], "streams", hop))
        return arrived

    def pick_in_order(layer, pieces):
        index = jnp.take(out_index.reshape(planes, room), (step - plane) % planes, axis=0, mode="clip")
        return pick(index.reshape(-1), pieces, layer, 1, planes * room)[0]

    def begin_at_once(part):
        far = [[p * group + j for p in range(planes)] for j in range(group)]
        return lax.all_to_all(
            part, "streams", split_axis=0, concat_axis=0, axis_index_groups=far, tiled=True
        )

    def finish(arrived):
        index = in_index
        if not isinstance(arrived, list):
            index = jnp.take(index.reshape(planes, room), (plane - step) % planes, axis=0, mode="clip")
            index, arrived = index.reshape(-1), [arrived]
        here = place(index, arrived, plane_slots).reshape(group, slots, rows, 128)
        return lax.all_to_all(
            here, "streams", split_axis=0, concat_axis=0, axis_index_groups=near, tiled=True
        )

    def settle(layer, got):
        got = lax.cond(fits, lambda x: x, lambda x: dense(layer), got)
        c = jnp.transpose(got[:, :, kv_rows:], (0, 2, 1, 3)).reshape(2, HALF, slots, 128)
        own = jnp.concatenate(
            [c[0, :taken], c[1, :taken, :, : convolution_cache.shape[3] - 128]], axis=-1
        )
        return got, own

    return packed, spread, pick_by_step, begin_by_steps, pick_in_order, begin_at_once, finish, settle


def attention_kernel(valid, order, bias, qkv, got, *rest):
    heads_out, kv_out, both, sorted_rows, packed = rest[-5:]
    group, slots, rows, lanes = got.shape
    heads = both.shape[1]
    kv_rows = heads * FR // group

    sorted_rows[...] = jnp.dot(
        order[...], qkv[...], preferred_element_type=jnp.float32
    ).astype(jnp.bfloat16)

    @pl.loop(0, slots)
    def _(s):
        for p in range(group):
            piece = got[p, s].astype(jnp.float32)
            for r in range(0, kv_rows, 8):
                q = p * kv_rows + r
                both[s, q // FR, q % FR : q % FR + 8, :] = piece[r : r + 8]
        new = sorted_rows[pl.ds(pl.multiple_of(s * CH, CH), CH), heads * lanes :]
        for h in range(heads):
            both[s, h, FR:, :] = new[:, h * lanes : (h + 1) * lanes].astype(jnp.float32)
            kv_out[s, 0, h] = both[s, h, pl.ds(valid[s], FR), :].astype(jnp.bfloat16)

    step = 4
    span = step * CH
    lane = lax.broadcasted_iota(jnp.int32, (span, lanes), 1)
    for g in range(slots // step):
        part = slice(g * span, (g + 1) * span)
        outs = []
        for h in range(heads):
            keys = both[g * step : (g + 1) * step, h].reshape(step * (FR + CH), lanes)
            keys = keys.astype(jnp.bfloat16)
            q = sorted_rows[part, h * lanes : (h + 1) * lanes]
            scores = lax.dot_general(
                q, keys, (((1,), (1,)), ((), ())), preferred_element_type=jnp.float32
            )
            scores = scores * HEAD_DIM ** (-0.5) + bias[part, :]
            peak = jnp.max(scores, axis=-1, keepdims=True)
            weights = jnp.exp(scores - peak)
            probs = (weights / jnp.sum(weights, axis=-1, keepdims=True)).astype(jnp.bfloat16)
            outs.append(jnp.dot(probs, keys, preferred_element_type=jnp.float32))
        first = jnp.where(lane < HEAD_DIM, pltpu.roll(outs[0], HEAD_DIM, 1), outs[1])
        second = pltpu.roll(outs[2], HEAD_DIM, 1)
        packed[part, :] = jnp.concatenate([first, second], axis=1).astype(jnp.bfloat16)
    back = lax.dot_general(
        order[...], packed[...], (((0,), (0,)), ((), ())), preferred_element_type=jnp.float32
    )
    heads_out[...] = back[:, : heads_out.shape[1]].astype(jnp.bfloat16)


def attention(layer, valid, order, bias, qkv, got, kv_so_far, heads):
    group, slots, rows, lanes = got.shape
    frames = qkv.shape[0]
    vmem = pl.BlockSpec(memory_space=pltpu.VMEM)
    more = [] if kv_so_far is None else [kv_so_far]
    return pl.pallas_call(
        attention_kernel,
        grid=(1,),
        in_specs=[pl.BlockSpec(memory_space=pltpu.SMEM)]
        + [vmem] * 4
        + [pl.BlockSpec(memory_space=pl.ANY)] * len(more),
        out_specs=[
            vmem,
            pl.BlockSpec((slots, 1, heads, FR, lanes), lambda i: (0, layer, 0, 0, 0)),
        ],
        out_shape=[
            jax.ShapeDtypeStruct((frames, heads * HEAD_DIM), jnp.bfloat16),
            jax.ShapeDtypeStruct((slots, LAYERS, heads, FR, lanes), jnp.bfloat16),
        ],
        scratch_shapes=[
            pltpu.VMEM((slots, heads, FR + CH, lanes), jnp.float32),
            pltpu.VMEM(qkv.shape, jnp.bfloat16),
            pltpu.VMEM((frames, 2 * lanes), jnp.bfloat16),
        ],
        input_output_aliases={5: 1} if more else {},
        compiler_params=pltpu.CompilerParams(vmem_limit_bytes=VMEM_LIMIT),
        name="attention",
    )(valid, order, bias, qkv, got, *more)


def silu(v):
    return v / (1.0 + jnp.exp(-v))


def block_kernel(last, place_of, state_in, valid, conv_gain, ffn_gain, next_gain, taps, cache, *rest):
    heads, (weights, tail), rest = rest[0:MP], rest[MP : MP + 2], rest[MP + 2 :]
    if last:
        result, new_conv, state, comb, own = rest
    else:
        state_out, result, new_conv, state, comb, own = rest
    frames, width = state_in.shape
    slots = frames // CH
    share = new_conv.shape[2]
    kept = KT - 1

    hidden_units = (weights.shape[1] - share) // 2
    total = state_in[...]
    for s, h in enumerate(heads):
        w = weights[(place_of[0] + s) % MP, :share, :]
        total = total + jnp.dot(h[...], w, preferred_element_type=jnp.float32)
    state[...] = total
    conv_in = norm(total, conv_gain[...])
    comb[kept:] = conv_in.astype(jnp.float32).reshape(CH, slots, width)
    comb[:kept] = cache[...].astype(jnp.float32)

    @pl.loop(0, width // 128)
    def _(c):
        lanes = pl.ds(pl.multiple_of(c * 128, 128), 128)
        for t in range(CH):
            mixed = taps[0:1, lanes] * comb[t, :, lanes]
            for k in range(1, KT):
                mixed = mixed + taps[k : k + 1, lanes] * comb[t + k, :, lanes]
            where = slice(t * slots, (t + 1) * slots)
            state[where, lanes] = state[where, lanes] + silu(mixed)

    for m in range(MP):

        @pl.when(place_of[0] == m)
        def _(m=m):
            own[...] = comb[:, :, m * share : (m + 1) * share]

    masks = [jnp.broadcast_to(valid[...] == v, (slots, share)) for v in range(1, CH + 1)]
    for j in range(kept):
        picked = own[j + 1]
        for v in range(2, CH + 1):
            picked = jnp.where(masks[v - 1], own[j + v], picked)
        new_conv[j] = picked.astype(jnp.bfloat16)

    total = state[...]
    ffn_in = norm(total, ffn_gain[...])
    for m in range(MP):
        up = weights[m, share : share + hidden_units, :]
        down = weights[m, share + hidden_units :, :]
        hidden = silu(
            lax.dot_general(
                ffn_in, up, (((1,), (1,)), ((), ())), preferred_element_type=jnp.float32
            )
        )
        total = total + jnp.dot(
            hidden.astype(jnp.bfloat16), down, preferred_element_type=jnp.float32
        )
    if last:
        rounded = total.astype(jnp.bfloat16)
        for m in range(MP):

            @pl.when(place_of[0] == m)
            def _(m=m):
                result[...] = lax.dot_general(
                    rounded[:, m * share : (m + 1) * share],
                    tail[...],
                    (((0,), (1,)), ((), ())),
                    preferred_element_type=jnp.float32,
                ).astype(jnp.bfloat16)

    else:
        state_out[...] = total
        result[...] = lax.dot_general(
            norm(total, next_gain[...]),
            tail[...],
            (((1,), (1,)), ((), ())),
            preferred_element_type=jnp.float32,
        ).astype(jnp.bfloat16)


def block(last, state, valid, gains, taps, cache, heads, weights, tail, share):
    frames, width = state.shape
    slots = frames // CH
    vmem = pl.BlockSpec(memory_space=pltpu.VMEM)
    place_of = lax.axis_index("mp").reshape(1)
    args = [state, valid, *gains, taps, cache, *heads, weights, tail]
    conv_shape = jax.ShapeDtypeStruct((KT - 1, slots, share), jnp.bfloat16)
    if last:
        shapes = [jax.ShapeDtypeStruct((share, frames), jnp.bfloat16), conv_shape]
    else:
        shapes = [
            jax.ShapeDtypeStruct((frames, width), jnp.float32),
            jax.ShapeDtypeStruct((frames, tail.shape[0]), jnp.bfloat16),
            conv_shape,
        ]
    return pl.pallas_call(
        functools.partial(block_kernel, last),
        in_specs=[pl.BlockSpec(memory_space=pltpu.SMEM)] + [vmem] * len(args),
        out_specs=[vmem] * len(shapes),
        out_shape=shapes,
        scratch_shapes=[
            pltpu.VMEM((frames, width), jnp.float32),
            pltpu.VMEM((KT - 1 + CH, slots, width), jnp.float32),
            pltpu.VMEM((KT - 1 + CH, slots, share), jnp.float32),
        ],
        compiler_params=pltpu.CompilerParams(vmem_limit_bytes=VMEM_LIMIT),
        name="block",
    )(place_of, *args)


def local(
    features,
    block_valid_frames,
    feature_running_mean,
    feature_running_variance,
    frames_counted,
    slot_relocation,
    speaker,
    speaker_adapter_row,
    adapter_down_panels,
    adapter_up_panels,
    input_weight,
    attention_norm_gain,
    query_key_value_weight,
    attention_output_weight,
    convolution_norm_gain,
    depthwise_taps,
    feedforward_norm_gain,
    up_weight,
    down_weight,
    key_value_cache,
    convolution_cache,
):
    slots = key_value_cache.shape[0]
    peers = lax.axis_size("streams")
    me = lax.axis_index("streams")
    mp = lax.axis_index("mp")
    first = me * slots
    held = adapter_down_panels.shape[0]
    width = input_weight.shape[1]
    heads = key_value_cache.shape[3]
    rows = slots * CH

    (
        packed,
        spread,
        pick_by_step,
        begin_by_steps,
        pick_in_order,
        begin_at_once,
        finish,
        settle,
    ) = move_caches(key_value_cache, convolution_cache, slot_relocation)

    small = jnp.concatenate(
        [
            attention_norm_gain,
            convolution_norm_gain,
            feedforward_norm_gain,
            depthwise_taps.reshape(LAYERS * KT, width),
        ],
        axis=0,
    )
    small, _ = lax.optimization_barrier((small, packed))
    small = side_by_side(ring(small))
    weights = []
    for l in range(LAYERS):
        mine = [attention_output_weight[l], jnp.transpose(up_weight[l]), down_weight[l]]
        weights.append(lax.all_gather(jnp.concatenate(mine, axis=0), "mp", axis=0))
    qkv_w = []
    for l in range(LAYERS):
        w = jnp.transpose(query_key_value_weight[l], (1, 2, 0))
        w = w.reshape(3, heads, HEAD_DIM, MODEL_WIDTH)
        pairs = jnp.stack(
            [
                jnp.stack([w[0], jnp.zeros_like(w[0])], axis=1),
                jnp.stack([w[1], w[2]], axis=1),
            ]
        )
        qkv_w.append(pairs.reshape(4 * heads * HEAD_DIM, MODEL_WIDTH))

    ids = jnp.arange(speaker_adapter_row.shape[0], dtype=jnp.int32)
    all_rows = jnp.sum(
        jnp.where(speaker[:, None] == ids[None, :], speaker_adapter_row[None, :], 0), axis=1
    )
    asked = all_rows.reshape(peers, slots)
    give = jnp.sum(jnp.where(asked // held == me, asked % held, 0), axis=1)
    my_rows = lax.dynamic_slice_in_dim(all_rows, first, slots, 0)
    flat_down = adapter_down_panels.reshape(held, -1, 128)
    flat_up = adapter_up_panels.reshape(held, -1, 128)
    panels = jnp.concatenate([flat_up, flat_down], axis=1)
    panels = jnp.take(panels, give, axis=0, mode="clip")
    spread, small = lax.optimization_barrier((spread, small))
    arrived = begin_by_steps(pick_by_step(0, spread))
    arrived[1], panels = lax.optimization_barrier((arrived[1], panels))
    got = exchange(panels)
    arrived, spread, weights[0] = lax.optimization_barrier((arrived, spread, weights[0]))
    attn_gain, conv_gain, ffn_gain = small[0:2], small[2:4], small[4:6]
    taps = small[6:].reshape(LAYERS, KT, MODEL_WIDTH)
    near_got = finish(arrived)
    second = pick_in_order(1, spread)
    got = jnp.take(got, my_rows // held, axis=0, mode="clip")
    panel_up = got[:, : flat_up.shape[1]].reshape((slots,) + adapter_up_panels.shape[1:])
    panel_down = got[:, flat_up.shape[1] :].reshape((slots,) + adapter_down_panels.shape[1:])

    frames = features.reshape(slots, CH, FILTER_CHANNELS)
    positions = jnp.arange(CH, dtype=jnp.int32)
    live = (positions[None, :] < block_valid_frames[:, None]).astype(jnp.float32)[:, :, None]
    seen_here = frames_counted[:, None]
    counted = seen_here + block_valid_frames.astype(jnp.float32)[:, None]
    new_mean = (seen_here * feature_running_mean + jnp.sum(live * frames, axis=1)) / counted
    centred = frames - new_mean[:, None, :]
    shifted = feature_running_mean - new_mean
    new_var = (
        seen_here * (feature_running_variance + shifted * shifted)
        + jnp.sum(live * centred * centred, axis=1)
    ) / counted
    normed = (centred / jnp.sqrt(new_var + CMVN_EPS)[:, None, :]).astype(jnp.bfloat16)
    low = jnp.einsum("stm,srm->str", normed, panel_down, preferred_element_type=jnp.float32).astype(
        jnp.bfloat16
    )
    part = dot(normed.reshape(rows, FILTER_CHANNELS), input_weight)
    part = part + jnp.einsum(
        "str,src->stc", low, panel_up, preferred_element_type=jnp.float32
    ).reshape(rows, width)
    part = jnp.transpose(part.reshape(slots, CH, width), (1, 0, 2)).reshape(rows, width)
    state = lax.all_gather(part, "mp", axis=1, tiled=True)

    row = jnp.arange(rows, dtype=jnp.int32)
    row_slot, row_frame = row // CH, row % CH
    order = (row[None, :] == (row_frame * slots + row_slot)[:, None]).astype(jnp.bfloat16)
    column = jnp.arange(4 * (FR + CH), dtype=jnp.int32)
    fresh = (column % (FR + CH) - FR)[None, :]
    allowed = (row_slot % 4)[:, None] == (column // (FR + CH))[None, :]
    row_valid = jnp.repeat(block_valid_frames, CH)[:, None]
    allowed = allowed & ((fresh < 0) | (fresh <= row_frame[:, None]) & (fresh < row_valid))
    bias = jnp.where(allowed, 0.0, -1e30).astype(jnp.float32)
    valid = block_valid_frames[:, None]

    qkv = lax.dot_general(
        norm(state, attn_gain[0]),
        qkv_w[0],
        (((1,), (1,)), ((), ())),
        preferred_element_type=jnp.float32,
    ).astype(jnp.bfloat16)
    near_got, second, state, qkv = lax.optimization_barrier((near_got, second, state, qkv))
    later = begin_at_once(second)
    kv_out = None
    conv_out = []
    for layer in range(LAYERS):
        last = layer == LAYERS - 1
        if last:
            later, state, qkv, weights[1] = lax.optimization_barrier(
                (later, state, qkv, weights[1])
            )
            near_got = finish(later)
        got, conv_own = settle(layer, near_got)
        heads_out, kv_out = attention(
            layer, block_valid_frames, order, bias, qkv, got, kv_out, heads
        )
        cache = side_by_side(ring(conv_own))
        following = 0 if last else layer + 1
        gains = [
            conv_gain[layer : layer + 1],
            ffn_gain[layer : layer + 1],
            attn_gain[following : following + 1],
        ]
        done = block(
            last,
            state,
            valid,
            gains,
            taps[layer],
            cache,
            ring(heads_out),
            weights[layer],
            order if last else qkv_w[layer + 1],
            width,
        )
        conv_out.append(done[-1])
        if last:
            enc_out = done[0]
        else:
            state, qkv = done[0], done[1]
    return (
        enc_out,
        jnp.transpose(kv_out, (0, 1, 3, 2, 4)),
        jnp.transpose(jnp.stack(conv_out), (2, 0, 1, 3)),
        new_mean,
        new_var,
    )


def solution(mesh):
    return jax.shard_map(
        local,
        mesh=mesh,
        in_specs=(
            P("streams", None),
            P("streams"),
            P("streams", None),
            P("streams", None),
            P("streams"),
            P(),
            P(),
            P(),
            P("streams", None, None),
            P("streams", None, "mp"),
            P(None, "mp"),
            P(None, "mp"),
            P(None, None, None, "mp"),
            P(None, "mp", None),
            P(None, "mp"),
            P(None, None, "mp"),
            P(None, "mp"),
            P(None, None, "mp"),
            P(None, "mp", None),
            P("streams", None, None, "mp", None),
            P("streams", None, None, "mp"),
        ),
        out_specs=(
            P("mp", "streams"),
            P("streams", None, None, "mp", None),
            P("streams", None, None, "mp"),
            P("streams", None),
            P("streams", None),
        ),
        check_vma=False,
    )
```
